128 devices in a mesh: head: 4 (over x_lo, core), ctx: 32 (over y, x_hi, z).
Axes of the slice: x: 4 (x_hi: 2, x_lo: 2; x = x_hi * 2 + x_lo), y: 4, z: 4, core: 2. Of those that a mesh axis runs over, the one named last changes fastest.
Arguments:
- keys: float32 [2, 6144, 4096], P(None, 'ctx', 'head'), may hold values from -6 to 6
- values: float32 [2, 6144, 4096], P(None, 'ctx', 'head'), may hold values from -6 to 6
- queries: float32 [2, 6144, 4096], P(None, 'ctx', 'head'), may hold values from -6 to 6
- rates: float32 [2, 6144], P(None, 'ctx'), may hold values from 0.05 to 1
- w_first: float32 [8, 512, 512], P('head'), may hold values from -0.25 to 0.25
- w_second: float32 [8, 512, 512], P('head'), may hold values from -0.25 to 0.25
- w_third: float32 [8, 512, 512], P('head'), may hold values from -0.25 to 0.25
- step_size: float32 [8], P('head'), may hold values from 0.2 to 1
- owner_order: int32 [32, 384], P('ctx'), may hold values from 0 to 383, each once within a row
- gate: float32 [32, 384, 4096], P('ctx', 'head'), may hold values from -6 to 6
- gain: float32 [4096], replicated, may hold values from 0.5 to 1.5
Outputs:
- mixed: float32 [32, 384, 4096], P('ctx', 'head')
The draws below stay inside these ranges and needn't reach their ends.
Inputs may be any that keep to these rules, and one draw needn't show every extreme that they name: Each row of owner_order is a permutation of the 384 tokens of its block.
All inputs are finite; a program needn't handle non-finite values.
Results may differ from the reference program's by a relative error of at most 0.0003.
Values sent between devices are 32-bit elements; how exact they have to be, the bound alone decides.
No kernel may reach another device: no remote copies, remote signals or barrier semaphores. Data moves between devices by JAX's collectives and lax.ppermute only.
A program may use at most 192 MiB of HBM per device.

```python
import math
import jax
import jax.numpy as jnp
from jax import lax

HD = 512
HEADS = 8
ROWS = 192
SPANS = 2
NS_STEPS = 5
WIDTH = 4096
SPAN = 6144
LOCAL = 384
N_CTX = 32


def steps_of(rng, dims, pieces, smallest, high):
    level = 1.0
    for position, shards_of in pieces:
        heights = jax.random.uniform(jax.random.fold_in(jax.random.fold_in(rng, 6), position), (shards_of,), jnp.float32, smallest / len(pieces), high / len(pieces))
        level = level * jnp.repeat(jnp.exp(heights), dims[position] // shards_of).reshape((-1,) + (1,) * (len(dims) - 1 - position))
    return level


def bell_draw(rng, dims, scale, bound, pieces=(), kind=jnp.bfloat16):
    loudness = steps_of(rng, dims, pieces, -0.22, 0.18) if pieces else 1.0
    drawn = jax.random.normal(rng, dims, jnp.float32) * scale * loudness
    return jnp.minimum(jnp.maximum(drawn, -bound), bound).astype(kind)


def setup_inputs(seed: int = 0) -> dict:
    key_list = jax.random.split(jax.random.key(seed), 12)
    return {
        "keys": bell_draw(key_list[0], (SPANS, SPAN, WIDTH), 1.0, 6.0, ((1, 32), (2, 4)), jnp.float32),
        "values": bell_draw(key_list[1], (SPANS, SPAN, WIDTH), 1.0, 6.0, ((1, 32), (2, 4)), jnp.float32),
        "queries": bell_draw(key_list[2], (SPANS, SPAN, WIDTH), 1.0, 6.0, ((1, 32), (2, 4)), jnp.float32),
        "rates": jnp.clip(jnp.exp(math.log(1.0) - 2.9957323 * jax.random.uniform(key_list[3], (SPANS, SPAN), jnp.float32) ** steps_of(key_list[3], (SPANS, SPAN), ((1, 32),), -0.2, 0.2)), 0.05, 1.0),
        "w_first": bell_draw(key_list[4], (HEADS, HD, HD), HD ** -0.5, 0.25, ((0, 4),), jnp.float32),
        "w_second": bell_draw(key_list[5], (HEADS, HD, HD), HD ** -0.5, 0.25, ((0, 4),), jnp.float32),
        "w_third": bell_draw(key_list[6], (HEADS, HD, HD), HD ** -0.5, 0.25, ((0, 4),), jnp.float32),
        "step_size": jnp.clip(jnp.exp(math.log(1.0) - 1.609438 * jax.random.uniform(key_list[7], (HEADS,), jnp.float32) ** steps_of(key_list[7], (HEADS,), ((0, 4),), -0.2, 0.2)), 0.2, 1.0),
        "owner_order": jax.vmap(lambda own: jax.random.permutation(own, LOCAL))(jax.random.split(key_list[8], N_CTX)).reshape((N_CTX, LOCAL)).astype(jnp.int32),
        "gate": bell_draw(key_list[9], (N_CTX, LOCAL, WIDTH), 1.0, 6.0, ((0, 32), (1, 4)), jnp.float32),
        "gain": jnp.clip(1.0 + 0.1 * jax.random.normal(key_list[10], (WIDTH,), jnp.float32), 0.5, 1.5),
    }


HIGH = lax.Precision.HIGHEST
COEFFS = (3.4445, -4.775, 2.0315)

def orthogonalize(matrix):
    scaled = matrix / (jnp.sqrt(lax.optimization_barrier(jnp.sum(matrix * matrix, axis=(-2, -1), keepdims=True))) + 1e-07)
    for repeat in range(NS_STEPS):
        square = jnp.einsum('...ij,...kj->...ik', scaled, scaled, precision=HIGH)
        blend = COEFFS[1] * square + COEFFS[2] * jnp.einsum('...ij,...jk->...ik', square, square, precision=HIGH)
        scaled = COEFFS[0] * scaled + jnp.einsum('...ij,...jk->...ik', blend, scaled, precision=HIGH)
    return scaled

def gradients(keys_now, values_now, rates_now, first_w, second_w, third_w):
    first = jnp.einsum('thd,hde->the', keys_now, first_w, precision=HIGH)
    third = jnp.einsum('thd,hde->the', keys_now, third_w, precision=HIGH)
    sigma = jax.nn.sigmoid(first)
    swish = first * sigma
    hidden = swish * third
    target = values_now * rates_now[:, None, None]
    grad_second = jnp.einsum('thd,the->hde', hidden, target, precision=HIGH)
    back = jnp.einsum('the,hde->thd', target, second_w, precision=HIGH)
    d_first = back * third * sigma * (1.0 + first * (1.0 - sigma))
    d_third = back * swish
    grad_first = jnp.einsum('thd,the->hde', keys_now, d_first, precision=HIGH)
    grad_third = jnp.einsum('thd,the->hde', keys_now, d_third, precision=HIGH)
    return jnp.stack([grad_first, grad_second, grad_third], axis=1)

def apply_fast(queries_now, first_w, second_w, third_w):
    first = jnp.einsum('thd,hde->the', queries_now, first_w, precision=HIGH)
    third = jnp.einsum('thd,hde->the', queries_now, third_w, precision=HIGH)
    hidden = jax.nn.silu(first) * third
    return jnp.einsum('thd,hde->the', hidden, second_w, precision=HIGH)

def reference(keys, values, queries, rates, w_first, w_second, w_third, step_size, owner_order, gate, gain):
    weights = jnp.stack([w_first, w_second, w_third], axis=1)
    eta = step_size[:, None, None, None]
    outputs = []
    for span in range(SPANS):
        keys_now = keys[span].reshape(SPAN, HEADS, HD)
        values_now = values[span].reshape(SPAN, HEADS, HD)
        queries_now = queries[span].reshape(SPAN, HEADS, HD)
        summed = gradients(keys_now, values_now, rates[span], weights[:, 0], weights[:, 1], weights[:, 2])
        weights = weights + eta * orthogonalize(summed)
        result = apply_fast(queries_now, weights[:, 0], weights[:, 1], weights[:, 2])
        outputs.append(result.reshape(SPAN, WIDTH))
    stacked = jnp.stack(outputs).reshape(SPANS, N_CTX, ROWS, WIDTH)
    blocks = jnp.transpose(stacked, (1, 0, 2, 3)).reshape(N_CTX, LOCAL, WIDTH)
    picked = jnp.take_along_axis(blocks, owner_order[:, :, None], axis=1)
    normed = picked * lax.rsqrt(lax.optimization_barrier(jnp.mean(picked * picked, axis=2, keepdims=True)) + 1e-06) * gain
    return normed * jax.nn.silu(gate)
```

```python
import jax
import jax.numpy as jnp
from jax import lax
from jax.sharding import Mesh, PartitionSpec as P

NS_STEPS = 5
COEFFS = (3.4445, -4.775, 2.0315)
HIGH = lax.Precision.HIGH
SPLIT = (("xl", 2), ("core", 2), ("y", 4), ("xh", 2), ("z", 4))
HEAD = ("xl", "core")
CTX = ("y", "xh", "z")
SIZES = dict(SPLIT)


def shift(value, axis, by):
    count = SIZES[axis]
    return lax.ppermute(value, axis, [(i, (i + by) % count) for i in range(count)])


def dot(left, right, spec):
    return jnp.einsum(spec, left, right, precision=HIGH, preferred_element_type=jnp.float32)


def orthogonalize(matrix):
    scaled = matrix / (jnp.sqrt(jnp.sum(matrix * matrix, axis=(-2, -1), keepdims=True)) + 1e-07)
    for _ in range(NS_STEPS):
        square = dot(scaled, scaled, "bij,bkj->bik")
        blend = COEFFS[1] * square + COEFFS[2] * dot(square, square, "bij,bjk->bik")
        scaled = COEFFS[0] * scaled + dot(blend, scaled, "bij,bjk->bik")
    return scaled


def gradients(keys, target, first_w, second_w, third_w):
    first = dot(keys, first_w, "td,de->te")
    third = dot(keys, third_w, "td,de->te")
    sigma = jax.nn.sigmoid(first)
    swish = first * sigma
    hidden = swish * third
    back = dot(target, second_w, "te,de->td")
    d_first = back * third * sigma * (1.0 + first * (1.0 - sigma))
    d_third = back * swish
    return jnp.stack(
        [
            dot(keys, d_first, "td,te->de"),
            dot(hidden, target, "td,te->de"),
            dot(keys, d_third, "td,te->de"),
        ]
    )


def apply_fast(queries, first_w, second_w, third_w):
    first = dot(queries, first_w, "td,de->te")
    third = dot(queries, third_w, "td,de->te")
    return dot(jax.nn.silu(first) * third, second_w, "td,de->te")


def sum_chunks(part, axis):
    count = SIZES[axis]
    here = lax.axis_index(axis)
    chunks = part.reshape(3, count, -1, part.shape[-1])

    def chunk(by):
        return lax.dynamic_index_in_dim(chunks, (here + by) % count, 1, keepdims=False)

    return chunk(0) + shift(chunk(1), axis, 1) + shift(chunk(3), axis, 3) + shift(chunk(2), axis, 2)


def sum_whole(part, axis):
    return part + shift(part, axis, 1) + shift(part, axis, 3) + shift(part, axis, 2)


def spread(part, axis):
    count = SIZES[axis]
    here = lax.axis_index(axis)
    held = jnp.stack([part, shift(part, axis, 1), shift(part, axis, 2), shift(part, axis, 3)])
    order = (here - jnp.arange(count)) % count
    return jnp.concatenate(
        [lax.dynamic_index_in_dim(held, order[q], 0, keepdims=False) for q in range(count)], axis=1
    )


def sum_plane(grads):
    half = grads.shape[1] // 2
    top, low = grads[:, :half], grads[:, half:]
    top, low = sum_chunks(top, "y"), sum_chunks(low, "z")
    top, low = sum_whole(top, "z"), sum_whole(low, "y")
    top, low = spread(top, "y"), spread(low, "z")
    return jnp.concatenate([top, low], axis=1)


def on_device(
    keys, values, queries, rates, w_first, w_second, w_third, step_size, owner_order, gate, gain
):
    size = w_first.shape[1]
    spans, rows = keys.shape[0], keys.shape[1]
    mine = lax.axis_index("xh")
    heads = SIZES["xl"] * SIZES["core"]

    def columns(array, which):
        return lax.dynamic_slice_in_dim(array, which * size, size, axis=-1)

    target = values * rates[:, :, None]
    pieces = [(keys, 0), (target, 0), (queries, 0), (keys, 1), (target, 1), (queries, 1)]
    kept = [columns(a[s], mine) for a, s in pieces]
    sent = [columns(a[s], 1 - mine) for a, s in pieces]
    came = list(shift(jnp.stack(sent[:2]), "xh", 1)) + list(shift(jnp.stack(sent[2:]), "xh", 1))
    both = [jnp.concatenate([a, b]) for a, b in zip(kept, came)]
    order = owner_order[0]
    other = shift(order, "xh", 1)

    weights = jnp.stack([w_first, w_second, w_third], axis=1)
    weights = lax.dynamic_index_in_dim(weights, mine, 0, keepdims=False)
    eta = lax.dynamic_index_in_dim(step_size, mine, 0, keepdims=False)
    outputs = []
    for span in range(spans):
        now = both[3 * span : 3 * span + 3]
        summed = sum_plane(gradients(now[0], now[1], weights[0], weights[1], weights[2]))
        weights = weights + eta * orthogonalize(summed)
        outputs.append(apply_fast(now[2], weights[0], weights[1], weights[2]))
    results = jnp.concatenate(outputs, axis=0)

    def place(tokens, block):
        return (tokens // rows) * (2 * rows) + block * rows + tokens % rows

    here, there = place(order, 0), place(other, 1)
    low = jnp.where(mine == 0, here, there).reshape(heads, 1, -1)
    high = jnp.where(mine == 0, there, here).reshape(heads, 1, -1)
    index = jnp.concatenate([low, high], axis=1).reshape(-1)
    picked = jnp.take(results, index, axis=0)
    regrouped = lax.all_to_all(picked, ("xl", "core", "xh"), split_axis=0, concat_axis=0, tiled=True)
    regrouped = regrouped.reshape(2 * heads, -1, size)
    total = jnp.sum(regrouped * regrouped, axis=(0, 2))
    scale = lax.rsqrt(total / (2 * heads * size) + 1e-06)
    whole = jnp.transpose(regrouped, (1, 0, 2)).reshape(-1, 2 * heads * size)
    return (whole * scale[:, None] * gain * jax.nn.silu(gate[0]))[None]


def solution(mesh):
    split = Mesh(
        mesh.devices.reshape([count for _, count in SPLIT]), [name for name, _ in SPLIT]
    )
    in_specs = (
        P(None, CTX, HEAD),
        P(None, CTX, HEAD),
        P(None, CTX, HEAD),
        P(None, CTX),
        P(HEAD, None, None),
        P(HEAD, None, None),
        P(HEAD, None, None),
        P(HEAD),
        P(CTX, None),
        P(CTX, HEAD, None),
        P(),
    )
    out_specs = P(CTX, HEAD, None)
    return jax.shard_map(
        on_device, mesh=split, in_specs=in_specs, out_specs=out_specs, check_vma=False
    )
```

```python
import jax
import jax.numpy as jnp
from jax import lax
from jax.sharding import Mesh, PartitionSpec as P

NS_STEPS = 5
COEFFS = (3.4445, -4.775, 2.0315)
HIGH = lax.Precision.HIGH
SPLIT = (("xl", 2), ("core", 2), ("y", 4), ("xh", 2), ("z", 4))
HEAD = ("xl", "core")
CTX = ("y", "xh", "z")
PLANE = ("y", "z")
CLASSES = 4
SIZES = dict(SPLIT)


def shift(value, axis, by):
    count = SIZES[axis]
    return lax.ppermute(value, axis, [(i, (i + by) % count) for i in range(count)])


def dot(left, right, spec):
    return jnp.einsum(spec, left, right, precision=HIGH, preferred_element_type=jnp.float32)


def orthogonalize(matrix):
    scaled = matrix / (jnp.sqrt(jnp.sum(matrix * matrix, axis=(-2, -1), keepdims=True)) + 1e-07)
    for _ in range(NS_STEPS):
        square = dot(scaled, scaled, "ij,kj->ik")
        blend = COEFFS[1] * square + COEFFS[2] * dot(square, square, "ij,jk->ik")
        scaled = COEFFS[0] * scaled + dot(blend, scaled, "ij,jk->ik")
    return scaled


def gradients(keys, target, first_w, second_w, third_w):
    first = dot(keys, first_w, "td,de->te")
    third = dot(keys, third_w, "td,de->te")
    sigma = jax.nn.sigmoid(first)
    swish = first * sigma
    hidden = swish * third
    back = dot(target, second_w, "te,de->td")
    d_first = back * third * sigma * (1.0 + first * (1.0 - sigma))
    d_third = back * swish
    return [
        dot(keys, d_first, "td,te->de"),
        dot(hidden, target, "td,te->de"),
        dot(keys, d_third, "td,te->de"),
    ]


def apply_fast(queries, first_w, second_w, third_w):
    first = dot(queries, first_w, "td,de->te")
    third = dot(queries, third_w, "td,de->te")
    return dot(jax.nn.silu(first) * third, second_w, "td,de->te")


def member(y, z):
    return (y + z) % CLASSES


def plane_shift(value, dy, dz, keep):
    pairs = []
    for y in range(CLASSES):
        for z in range(CLASSES):
            if keep(y, z):
                there = ((y + dy) % CLASSES) * CLASSES + (z + dz) % CLASSES
                pairs.append((y * CLASSES + z, there))
    return lax.ppermute(value, PLANE, pairs)


def pick(array, index, axis):
    return lax.dynamic_index_in_dim(array, index, axis, keepdims=False)


def choose(which, options):
    result = options[-1]
    for number in range(len(options) - 2, -1, -1):
        result = jnp.where(which == number, options[number], result)
    return result


def updates_of(grads):
    size = grads[0].shape[0]
    half, row = size // 2, size // 2 // CLASSES
    y, z = lax.axis_index("y"), lax.axis_index("z")
    mine = member(y, z)
    always = lambda *_: True
    steps = (1, 3, 2)

    def chunk(first, index):
        return jnp.stack([lax.dynamic_slice_in_dim(g, first + index * row, row, 0) for g in grads])

    tops = [chunk(0, (y + d) % CLASSES) for d in (0,) + steps]
    lows = [chunk(half, (z + d) % CLASSES) for d in (0,) + steps]
    top, low = tops[0], lows[0]
    for number, d in enumerate(steps):
        top = top + plane_shift(tops[number + 1], d, 0, always)
        low = low + plane_shift(lows[number + 1], 0, d, always)
    matrix = lambda d: jnp.minimum((mine + d) % CLASSES, 2)
    top_sum, low_sum = pick(top, matrix(0), 0), pick(low, matrix(0), 0)
    for d in steps:
        used = lambda a, b: member(a, b + d) < 3
        top_sum = top_sum + plane_shift(pick(top, matrix(d), 0), 0, d, used)
        low_sum = low_sum + plane_shift(pick(low, matrix(d), 0), d, 0, used)
    held = jnp.stack([top_sum, low_sum])
    whose = lambda a, b: member(a, b) < 3
    ring = jnp.stack([held] + [plane_shift(held, d, -d, whose) for d in (1, 2, 3)])
    parts = [ring[:, 0], ring[:, 1]]
    rows_top = [pick(parts[0], (y - q) % CLASSES, 0) for q in range(CLASSES)]
    rows_low = [pick(parts[1], (q - z) % CLASSES, 0) for q in range(CLASSES)]
    update = orthogonalize(jnp.concatenate(rows_top + rows_low, axis=0))
    tops, lows = [update[:half]], [update[half:]]
    for d in (1, 2, 3):
        tops.append(plane_shift(update[:half], d, 0, whose))
        lows.append(plane_shift(update[half:], 0, d, whose))
    return [
        jnp.concatenate([choose((mine - m) % CLASSES, part) for part in (tops, lows)], axis=0)
        for m in range(3)
    ]


def on_device(
    keys, values, queries, rates, w_first, w_second, w_third, step_size, owner_order, gate, gain
):
    size = w_first.shape[1]
    spans, rows = keys.shape[0], keys.shape[1]
    mine = lax.axis_index("xh")
    heads = SIZES["xl"] * SIZES["core"]

    def columns(array, which):
        return lax.dynamic_slice_in_dim(array, which * size, size, axis=-1)

    target = values * rates[:, :, None]
    pieces = [(keys, 0), (target, 0), (queries, 0), (keys, 1), (target, 1), (queries, 1)]
    kept = [columns(a[s], mine) for a, s in pieces]
    sent = [columns(a[s], 1 - mine) for a, s in pieces]
    came = [shift(sent[0], "xh", 1), shift(sent[1], "xh", 1)]
    later, came[0], came[1], order = lax.optimization_barrier(
        (jnp.stack(sent[2:]), came[0], came[1], owner_order[0])
    )
    came = came + list(shift(later, "xh", 1))
    both = [jnp.concatenate([a, b]) for a, b in zip(kept, came)]
    other = shift(order, "xh", 1)

    weights = [
        lax.dynamic_index_in_dim(w, mine, 0, keepdims=False) for w in (w_first, w_second, w_third)
    ]
    eta = lax.dynamic_index_in_dim(step_size, mine, 0, keepdims=False)
    outputs = []
    for span in range(spans):
        now = both[3 * span : 3 * span + 3]
        updates = updates_of(gradients(now[0], now[1], weights[0], weights[1], weights[2]))
        weights = [w + eta * u for w, u in zip(weights, updates)]
        outputs.append(apply_fast(now[2], weights[0], weights[1], weights[2]))
    results = jnp.concatenate(outputs, axis=0)

    def place(tokens, block):
        return (tokens // rows) * (2 * rows) + block * rows + tokens % rows

    here, there = place(order, 0), place(other, 1)
    low = jnp.where(mine == 0, here, there).reshape(heads, 1, -1)
    high = jnp.where(mine == 0, there, here).reshape(heads, 1, -1)
    index = jnp.concatenate([low, high], axis=1).reshape(-1)
    picked = jnp.take(results, index, axis=0)
    regrouped = lax.all_to_all(picked, ("xl", "core", "xh"), split_axis=0, concat_axis=0, tiled=True)
    regrouped = regrouped.reshape(2 * heads, -1, size)
    total = jnp.sum(regrouped * regrouped, axis=(0, 2))
    scale = lax.rsqrt(total / (2 * heads * size) + 1e-06)
    whole = jnp.transpose(regrouped, (1, 0, 2)).reshape(-1, 2 * heads * size)
    return (whole * scale[:, None] * gain * jax.nn.silu(gate[0]))[None]


def solution(mesh):
    split = Mesh(
        mesh.devices.reshape([count for _, count in SPLIT]), [name for name, _ in SPLIT]
    )
    in_specs = (
        P(None, CTX, HEAD),
        P(None, CTX, HEAD),
        P(None, CTX, HEAD),
        P(None, CTX),
        P(HEAD, None, None),
        P(HEAD, None, None),
        P(HEAD, None, None),
        P(HEAD),
        P(CTX, None),
        P(CTX, HEAD, None),
        P(),
    )
    out_specs = P(CTX, HEAD, None)
    return jax.shard_map(
        on_device, mesh=split, in_specs=in_specs, out_specs=out_specs, check_vma=False
    )
```

```python
import jax
import jax.numpy as jnp
from jax import lax
from jax.experimental import pallas as pl
from jax.experimental.pallas import tpu as pltpu
from jax.sharding import Mesh, PartitionSpec as P

NS_STEPS = 5
COEFFS = (3.4445, -4.775, 2.0315)
HIGH = lax.Precision.HIGH
SPLIT = (("xl", 2), ("core", 2), ("y", 4), ("xh", 2), ("z", 4))
HEAD = ("xl", "core")
CTX = ("y", "xh", "z")
SIZES = dict(SPLIT)
RING = 4
STEPS = (2, 1, 3)
F32, BF16 = jnp.float32, jnp.bfloat16
VMEM = pl.BlockSpec(memory_space=pltpu.VMEM)
SMEM = pl.BlockSpec(memory_space=pltpu.SMEM)
PARAMS = pltpu.CompilerParams(vmem_limit_bytes=50 * 2**20)


def shift(value, axis, by):
    count = SIZES[axis]
    return lax.ppermute(value, axis, [(i, (i + by) % count) for i in range(count)])


def dot(left, right, spec):
    return jnp.einsum(spec, left, right, precision=HIGH, preferred_element_type=F32)


def halves(value):
    high = value.astype(BF16)
    return high, (value - high.astype(F32)).astype(BF16)


def product(left, right, left_dim=1, right_dim=0):
    def one(a, b):
        return lax.dot_general(
            a, b, (((left_dim,), (right_dim,)), ((), ())), preferred_element_type=F32
        )

    return one(left[0], right[0]) + (one(left[0], right[1]) + one(left[1], right[0]))


def gradient_kernel(place, k_own, k_came, t_own, t_came, w1, w2, w3, *rest):
    tops, lows, grads = rest[:RING], rest[RING : 2 * RING], rest[2 * RING]
    size = w1.shape[0]
    keys = halves(jnp.concatenate([k_own[...], k_came[...]], axis=0))
    target = halves(jnp.concatenate([t_own[...], t_came[...]], axis=0))
    first = product(keys, halves(w1[...]))
    third = product(keys, halves(w3[...]))
    sigma = jax.nn.sigmoid(first)
    swish = first * sigma
    grads[1] = product(halves(swish * third), target, 0, 0)
    back = product(target, halves(w2[...]), 1, 1)
    grads[2] = product(keys, halves(back * swish), 0, 0)
    d_first = back * third * sigma * (1.0 + first * (1.0 - sigma))
    grads[0] = product(keys, halves(d_first), 0, 0)
    row = size // 2 // RING
    for d in range(RING):
        top = pl.multiple_of(((place[0] + d) & (RING - 1)) * row, row)
        low = pl.multiple_of(((place[1] + d) & (RING - 1)) * row + size // 2, row)
        tops[d][...] = grads[:, pl.ds(top, row), :]
        lows[d][...] = grads[:, pl.ds(low, row), :]


def gradients(place, keys, target, weights):
    size = weights[0].shape[0]
    rows = 2 * keys[0].shape[0]
    chunk = jax.ShapeDtypeStruct((3, size // 2 // RING, size), F32)
    out = pl.pallas_call(
        gradient_kernel,
        out_shape=[chunk] * (2 * RING),
        in_specs=[SMEM] + [VMEM] * 7,
        out_specs=[VMEM] * (2 * RING),
        scratch_shapes=[pltpu.VMEM((3, size, size), F32)],
        compiler_params=PARAMS,
        cost_estimate=pl.CostEstimate(
            flops=36 * rows * size * size, bytes_accessed=32 * size * size, transcendentals=rows * size
        ),
        name="gradients",
    )(place, *keys, *target, *weights)
    return out[:RING], out[RING:]


def update_kernel(place, eta, *refs):
    tops, lows, weights, outs = refs[:RING], refs[RING : 2 * RING], refs[8:11], refs[11:14]
    x, xh, xl, ah, al, bh, bl = refs[14:]
    size = x.shape[1]
    row, half = size // 2 // RING, size // 2
    for number, d in enumerate((0,) + STEPS):
        top = pl.multiple_of(((place[0] - d) & (RING - 1)) * row, row)
        low = pl.multiple_of(((place[1] - d) & (RING - 1)) * row + half, row)
        x[:, pl.ds(top, row), :] = tops[number][...]
        x[:, pl.ds(low, row), :] = lows[number][...]
    for m in range(3):
        g = x[m]
        scaled = g / (jnp.sqrt(jnp.sum(g * g)) + 1e-07)
        x[m] = scaled
        xh[m], xl[m] = halves(scaled)

    def part(i):
        return slice(i * half, (i + 1) * half)

    def rows(pair, m, i):
        return tuple(ref[m, part(i), :] for ref in pair)

    def columns(pair, m, j):
        return tuple(ref[m, :, part(j)] for ref in pair)

    def block(pair, m, i, j):
        return pair[0][m, part(i), part(j)].astype(F32) + pair[1][m, part(i), part(j)].astype(F32)

    def symmetric(pair, m, make):
        for i, j in ((0, 1), (0, 0), (1, 1)):
            for ref, piece in zip(pair, halves(make(i, j))):
                ref[m, part(i), part(j)] = piece
        for ref in pair:
            ref[m, part(1), part(0)] = ref[m, part(0), part(1)].T

    xs, squares, blends = (xh, xl), (ah, al), (bh, bl)

    def step(_, carry):
        for m in range(3):
            symmetric(
                squares, m, lambda i, j: product(rows(xs, m, i), rows(xs, m, j), 1, 1)
            )
        for m in range(3):
            symmetric(
                blends,
                m,
                lambda i, j: COEFFS[1] * block(squares, m, i, j)
                + COEFFS[2] * product(rows(squares, m, i), columns(squares, m, j)),
            )
        for m in range(3):
            new = COEFFS[0] * x[m] + product((bh[m], bl[m]), (xh[m], xl[m]))
            x[m] = new
            xh[m], xl[m] = halves(new)
        return carry

    lax.fori_loop(0, NS_STEPS, step, 0)
    for m in range(3):
        outs[m][...] = weights[m][...] + eta[0] * x[m]


def update(place, eta, tops, lows, weights):
    size = weights[0].shape[0]
    return pl.pallas_call(
        update_kernel,
        out_shape=[jax.ShapeDtypeStruct((size, size), F32)] * 3,
        in_specs=[SMEM, SMEM] + [VMEM] * (2 * RING + 3),
        out_specs=[VMEM] * 3,
        scratch_shapes=[pltpu.VMEM((3, size, size), F32)] + [pltpu.VMEM((3, size, size), BF16)] * 6,
        compiler_params=PARAMS,
        cost_estimate=pl.CostEstimate(
            flops=3 * 15 * 6 * size**3, bytes_accessed=36 * size * size, transcendentals=0
        ),
        name="update",
    )(place, eta, *tops, *lows, *weights)


def finish_kernel(picked, gate, gain, out):
    heads, _, size = picked.shape
    total = sum(jnp.sum(picked[h] * picked[h], axis=1, keepdims=True) for h in range(heads))
    scale = lax.rsqrt(total / (heads * size) + 1e-06)
    for h in range(heads):
        here = slice(h * size, (h + 1) * size)
        now = gate[:, here]
        out[:, here] = picked[h] * scale * gain[:, here] * (now * jax.nn.sigmoid(now))


def finish(picked, gate, gain):
    return pl.pallas_call(
        finish_kernel,
        out_shape=jax.ShapeDtypeStruct(gate.shape, F32),
        in_specs=[VMEM] * 3,
        out_specs=VMEM,
        compiler_params=PARAMS,
        cost_estimate=pl.CostEstimate(
            flops=8 * gate.size, bytes_accessed=12 * gate.size, transcendentals=gate.size
        ),
        name="finish",
    )(picked, gate, gain)


def apply_fast(queries, first_w, second_w, third_w):
    first = dot(queries, first_w, "td,de->te")
    third = dot(queries, third_w, "td,de->te")
    return dot(jax.nn.silu(first) * third, second_w, "td,de->te")


def sum_plane(tops, lows):
    top, low = tops[0], lows[0]
    came = [(shift(tops[d], "y", d), shift(lows[d], "z", d)) for d in STEPS]
    for a, b in came:
        top, low = top + a, low + b
    came = [(shift(top, "z", d), shift(low, "y", d)) for d in STEPS]
    for a, b in came:
        top, low = top + a, low + b
    came = [(shift(top, "y", d), shift(low, "z", d)) for d in STEPS]
    return [top] + [a for a, _ in came], [low] + [b for _, b in came]


def on_device(
    keys, values, queries, rates, w_first, w_second, w_third, step_size, owner_order, gate, gain
):
    size = w_first.shape[1]
    spans, rows = keys.shape[0], keys.shape[1]
    mine = lax.axis_index("xh")
    low_side = mine == 0
    heads = SIZES["xl"] * SIZES["core"]
    place = jnp.stack([lax.axis_index("y"), lax.axis_index("z")]).astype(jnp.int32)

    def sides(array):
        left, right = array[:, :size], array[:, size:]
        return jnp.where(low_side, left, right), jnp.where(low_side, right, left)

    def swapped(array):
        kept, sent = sides(array)
        return kept, shift(sent, "xh", 1)

    now_keys = swapped(keys[0])
    now_target = swapped(values[0] * rates[0][:, None])
    pieces = [queries[0]] + [
        piece for s in range(1, spans) for piece in (keys[s], values[s] * rates[s][:, None], queries[s])
    ]
    kept, sent = zip(*[sides(piece) for piece in pieces])
    order = owner_order[0]
    later, order, *first_came = lax.optimization_barrier(
        (jnp.stack(sent), order, now_keys[1], now_target[1])
    )
    now_keys, now_target = (now_keys[0], first_came[0]), (now_target[0], first_came[1])
    came = shift(later, "xh", 1)
    other = shift(order, "xh", 1)
    pairs = [(kept[n], came[n]) for n in range(len(kept))]

    weights = [jnp.where(low_side, w[0], w[1]) for w in (w_first, w_second, w_third)]
    eta = jnp.where(low_side, step_size[:1], step_size[1:])
    outputs = []
    for span in range(spans):
        if span:
            now_keys, now_target = pairs[3 * span - 2], pairs[3 * span - 1]
        tops, lows = sum_plane(*gradients(place, now_keys, now_target, weights))
        weights = update(place, eta, tops, lows, weights)
        outputs.append(apply_fast(jnp.concatenate(pairs[3 * span]), *weights))
    results = jnp.concatenate(outputs, axis=0)

    def locate(tokens, block):
        return (tokens // rows) * (2 * rows) + block * rows + tokens % rows

    here, there = locate(order, 0), locate(other, 1)
    low = jnp.where(low_side, here, there).reshape(heads, 1, -1)
    high = jnp.where(low_side, there, here).reshape(heads, 1, -1)
    index = jnp.concatenate([low, high], axis=1).reshape(-1)
    picked = jnp.take(results, index, axis=0)
    regrouped = lax.all_to_all(picked, ("xl", "core", "xh"), split_axis=0, concat_axis=0, tiled=True)
    return finish(regrouped.reshape(2 * heads, -1, size), gate[0], gain[None])[None]


def solution(mesh):
    split = Mesh(
        mesh.devices.reshape([count for _, count in SPLIT]), [name for name, _ in SPLIT]
    )
    in_specs = (
        P(None, CTX, HEAD),
        P(None, CTX, HEAD),
        P(None, CTX, HEAD),
        P(None, CTX),
        P(HEAD, None, None),
        P(HEAD, None, None),
        P(HEAD, None, None),
        P(HEAD),
        P(CTX, None),
        P(CTX, HEAD, None),
        P(),
    )
    out_specs = P(CTX, HEAD, None)
    return jax.shard_map(
        on_device, mesh=split, in_specs=in_specs, out_specs=out_specs, check_vma=False
    )
```

```python
import jax
import jax.numpy as jnp
from jax import lax
from jax.experimental import pallas as pl
from jax.experimental.pallas import tpu as pltpu
from jax.sharding import Mesh, PartitionSpec as P

NS_STEPS = 5
COEFFS = (3.4445, -4.775, 2.0315)
HIGH = lax.Precision.HIGH
SPLIT = (("xl", 2), ("core", 2), ("y", 4), ("xh", 2), ("z", 4))
HEAD = ("xl", "core")
CTX = ("y", "xh", "z")
SIZES = dict(SPLIT)
RING = 4
STEPS = (2, 1, 3)
F32, BF16 = jnp.float32, jnp.bfloat16
VMEM = pl.BlockSpec(memory_space=pltpu.VMEM)
SMEM = pl.BlockSpec(memory_space=pltpu.SMEM)
PARAMS = pltpu.CompilerParams(vmem_limit_bytes=50 * 2**20)


def shift(value, axis, by):
    count = SIZES[axis]
    return lax.ppermute(value, axis, [(i, (i + by) % count) for i in range(count)])


def dot(left, right, spec):
    return jnp.einsum(spec, left, right, precision=HIGH, preferred_element_type=F32)


def halves(value):
    high = value.astype(BF16)
    return high, (value - high.astype(F32)).astype(BF16)


def product(left, right, left_dim=1, right_dim=0):
    def one(a, b):
        return lax.dot_general(
            a, b, (((left_dim,), (right_dim,)), ((), ())), preferred_element_type=F32
        )

    return one(left[0], right[0]) + (one(left[0], right[1]) + one(left[1], right[0]))


def gradient_chunks(place, keys, target, w1, w2, w3, tops, lows, grads):
    size = w1.shape[0]
    keys, target = halves(keys), halves(target)
    first = product(keys, halves(w1[...]))
    third = product(keys, halves(w3[...]))
    sigma = jax.nn.sigmoid(first)
    swish = first * sigma
    grads[1] = product(halves(swish * third), target, 0, 0)
    back = product(target, halves(w2[...]), 1, 1)
    grads[2] = product(keys, halves(back * swish), 0, 0)
    d_first = back * third * sigma * (1.0 + first * (1.0 - sigma))
    grads[0] = product(keys, halves(d_first), 0, 0)
    row = size // 2 // RING
    for d in range(RING):
        top = pl.multiple_of(((place[0] + d) & (RING - 1)) * row, row)
        low = pl.multiple_of(((place[1] + d) & (RING - 1)) * row + size // 2, row)
        tops[d][...] = grads[:, pl.ds(top, row), :]
        lows[d][...] = grads[:, pl.ds(low, row), :]


def add_updates(place, eta, updates, weights, outs):
    kind = place[0] + place[1]
    for m in range(3):
        for e in range(RING):

            @pl.when(((m - kind) & (RING - 1)) == e)
            def _(m=m, e=e):
                outs[m][...] = weights[m][...] + eta[0] * updates[e][...]


def first_kernel(place, k_own, k_came, t_own, t_came, w1, w2, w3, *rest):
    keys = jnp.concatenate([k_own[...], k_came[...]], axis=0)
    target = jnp.concatenate([t_own[...], t_came[...]], axis=0)
    gradient_chunks(place, keys, target, w1, w2, w3, rest[:RING], rest[RING : 2 * RING], rest[2 * RING])


def next_kernel(place, eta, k_own, k_came, t_own, t_came, *refs):
    updates, weights, outs = refs[:RING], refs[4:7], refs[7:10]
    tops, lows, grads = refs[10 : 10 + RING], refs[10 + RING : 10 + 2 * RING], refs[10 + 2 * RING]
    add_updates(place, eta, updates, weights, outs)
    keys = jnp.concatenate([k_own[...], k_came[...]], axis=0)
    target = jnp.concatenate([t_own[...], t_came[...]], axis=0)
    gradient_chunks(place, keys, target, *outs, tops, lows, grads)


def last_kernel(place, eta, q_own, q_came, *refs):
    updates, weights, result, held = refs[:RING], refs[4:7], refs[7], refs[8:]
    add_updates(place, eta, updates, weights, held)
    queries = halves(jnp.concatenate([q_own[...], q_came[...]], axis=0))
    first = product(queries, halves(held[0][...]))
    third = product(queries, halves(held[2][...]))
    result[...] = product(halves(first * jax.nn.sigmoid(first) * third), halves(held[1][...]))


def gradient_cost(rows, size):
    return pl.CostEstimate(
        flops=36 * rows * size * size, bytes_accessed=32 * size * size, transcendentals=rows * size
    )


def gradients(place, keys, target, weights):
    size = weights[0].shape[0]
    chunk = jax.ShapeDtypeStruct((3, size // 2 // RING, size), F32)
    out = pl.pallas_call(
        first_kernel,
        out_shape=[chunk] * (2 * RING),
        in_specs=[SMEM] + [VMEM] * 7,
        out_specs=[VMEM] * (2 * RING),
        scratch_shapes=[pltpu.VMEM((3, size, size), F32)],
        compiler_params=PARAMS,
        cost_estimate=gradient_cost(2 * keys[0].shape[0], size),
        name="gradients",
    )(place, *keys, *target, *weights)
    return out[:RING], out[RING:]


def update_and_gradients(place, eta, keys, target, updates, weights):
    size = weights[0].shape[0]
    chunk = jax.ShapeDtypeStruct((3, size // 2 // RING, size), F32)
    square = jax.ShapeDtypeStruct((size, size), F32)
    out = pl.pallas_call(
        next_kernel,
        out_shape=[square] * 3 + [chunk] * (2 * RING),
        in_specs=[SMEM, SMEM] + [VMEM] * (RING + 7),
        out_specs=[VMEM] * (3 + 2 * RING),
        scratch_shapes=[pltpu.VMEM((3, size, size), F32)],
        compiler_params=PARAMS,
        cost_estimate=gradient_cost(2 * keys[0].shape[0], size),
        name="update_and_gradients",
    )(place, eta, *keys, *target, *updates, *weights)
    return out[:3], out[3 : 3 + RING], out[3 + RING :]


def update_and_apply(place, eta, queries, updates, weights):
    size = weights[0].shape[0]
    rows = 2 * queries[0].shape[0]
    return pl.pallas_call(
        last_kernel,
        out_shape=jax.ShapeDtypeStruct((rows, size), F32),
        in_specs=[SMEM, SMEM] + [VMEM] * (RING + 5),
        out_specs=VMEM,
        scratch_shapes=[pltpu.VMEM((size, size), F32)] * 3,
        compiler_params=PARAMS,
        cost_estimate=pl.CostEstimate(
            flops=18 * rows * size * size, bytes_accessed=32 * size * size, transcendentals=rows * size
        ),
        name="update_and_apply",
    )(place, eta, *queries, *updates, *weights)


def pick_kernel(place, own, *refs):
    came, outs = refs[: RING - 1], refs[RING - 1 :]
    kind = place[0] + place[1]
    for d in range(RING):
        matrix = jnp.minimum((kind + d) & (RING - 1), 2)
        outs[d][...] = own[matrix] + (came[0][matrix] + (came[1][matrix] + came[2][matrix]))


def pick(place, own, came):
    chunk = jax.ShapeDtypeStruct(own.shape[1:], F32)
    return pl.pallas_call(
        pick_kernel,
        out_shape=[chunk] * RING,
        in_specs=[SMEM] + [VMEM] * RING,
        out_specs=[VMEM] * RING,
        compiler_params=PARAMS,
        cost_estimate=pl.CostEstimate(
            flops=4 * own.size, bytes_accessed=22 * own.size, transcendentals=0
        ),
        name="pick",
    )(place, own, *came)


def orthogonal_kernel(place, *refs):
    chunks, out, (x, xh, xl, ah, al, bh, bl) = refs[:RING], refs[4], refs[5:]
    size = x.shape[0]
    row, half = size // 2 // RING, size // 2
    for d in range(RING):
        top = pl.multiple_of(((place[0] - d) & (RING - 1)) * row, row)
        low = pl.multiple_of(((place[1] + d) & (RING - 1)) * row + half, row)
        x[pl.ds(top, row), :] = chunks[d][0]
        x[pl.ds(low, row), :] = chunks[d][1]
    g = x[...]
    scaled = g / (jnp.sqrt(jnp.sum(g * g)) + 1e-07)
    x[...] = scaled
    xh[...], xl[...] = halves(scaled)

    def part(i):
        return slice(i * half, (i + 1) * half)

    def rows(pair, i):
        return tuple(ref[part(i), :] for ref in pair)

    def columns(pair, j):
        return tuple(ref[:, part(j)] for ref in pair)

    def block(pair, i, j):
        return pair[0][part(i), part(j)].astype(F32) + pair[1][part(i), part(j)].astype(F32)

    def symmetric(pair, make):
        for i, j in ((0, 1), (0, 0), (1, 1)):
            for ref, piece in zip(pair, halves(make(i, j))):
                ref[part(i), part(j)] = piece
        for ref in pair:
            ref[part(1), part(0)] = ref[part(0), part(1)].T

    xs, squares, blends = (xh, xl), (ah, al), (bh, bl)

    def step(_, carry):
        symmetric(squares, lambda i, j: product(rows(xs, i), rows(xs, j), 1, 1))
        symmetric(
            blends,
            lambda i, j: COEFFS[1] * block(squares, i, j)
            + COEFFS[2] * product(rows(squares, i), columns(squares, j)),
        )
        new = COEFFS[0] * x[...] + product((bh[...], bl[...]), (xh[...], xl[...]))
        x[...] = new
        xh[...], xl[...] = halves(new)
        return carry

    lax.fori_loop(0, NS_STEPS, step, 0)
    out[...] = x[...]


def orthogonal(place, chunks):
    size = chunks[0].shape[-1]
    return pl.pallas_call(
        orthogonal_kernel,
        out_shape=jax.ShapeDtypeStruct((size, size), F32),
        in_specs=[SMEM] + [VMEM] * RING,
        out_specs=VMEM,
        scratch_shapes=[pltpu.VMEM((size, size), F32)] + [pltpu.VMEM((size, size), BF16)] * 6,
        compiler_params=PARAMS,
        cost_estimate=pl.CostEstimate(
            flops=15 * 6 * size**3, bytes_accessed=8 * size * size, transcendentals=0
        ),
        name="orthogonal",
    )(place, *chunks)


def finish_kernel(picked, gate, gain, out):
    heads, _, size = picked.shape
    total = sum(jnp.sum(picked[h] * picked[h], axis=1, keepdims=True) for h in range(heads))
    scale = lax.rsqrt(total / (heads * size) + 1e-06)
    for h in range(heads):
        here = slice(h * size, (h + 1) * size)
        now = gate[:, here]
        out[:, here] = picked[h] * scale * gain[:, here] * (now * jax.nn.sigmoid(now))


def finish(picked, gate, gain):
    return pl.pallas_call(
        finish_kernel,
        out_shape=jax.ShapeDtypeStruct(gate.shape, F32),
        in_specs=[VMEM] * 3,
        out_specs=VMEM,
        compiler_params=PARAMS,
        cost_estimate=pl.CostEstimate(
            flops=8 * gate.size, bytes_accessed=12 * gate.size, transcendentals=gate.size
        ),
        name="finish",
    )(picked, gate, gain)


def apply_fast(queries, first_w, second_w, third_w):
    first = dot(queries, first_w, "td,de->te")
    third = dot(queries, third_w, "td,de->te")
    return dot(jax.nn.silu(first) * third, second_w, "td,de->te")


def plane_shift(value, dy, dz, used=lambda y, z: True):
    pairs = [
        (y * RING + z, (y + dy) % RING * RING + (z + dz) % RING)
        for y in range(RING)
        for z in range(RING)
        if used(y, z)
    ]
    return lax.ppermute(value, ("y", "z"), pairs)


def sum_to_diagonals(place, tops, lows):
    top_came = [plane_shift(tops[d], d, 0) for d in STEPS]
    low_came = [plane_shift(lows[d], 0, d) for d in STEPS]
    tops, lows = pick(place, tops[0], top_came), pick(place, lows[0], low_came)
    top, low = tops[0], lows[0]
    for d in STEPS:
        top = top + plane_shift(tops[d], 0, d)
        low = low + plane_shift(lows[d], d, 0)
    held = jnp.stack([top, low])
    return [held] + [plane_shift(held, d, -d) for d in range(1, RING)]


def share(update):
    used = lambda y, z: (y + z) % RING < 3
    opposite = plane_shift(update, RING // 2, 0, used)
    return [update, plane_shift(update, 0, -1, used), opposite, plane_shift(update, 0, 1, used)]


def on_device(
    keys, values, queries, rates, w_first, w_second, w_third, step_size, owner_order, gate, gain
):
    size = w_first.shape[1]
    spans, rows = keys.shape[0], keys.shape[1]
    mine = lax.axis_index("xh")
    low_side = mine == 0
    heads = SIZES["xl"] * SIZES["core"]
    place = jnp.stack([lax.axis_index("y"), lax.axis_index("z")]).astype(jnp.int32)

    def sides(array):
        left, right = array[:, :size], array[:, size:]
        return jnp.where(low_side, left, right), jnp.where(low_side, right, left)

    def swapped(array):
        kept, sent = sides(array)
        return kept, shift(sent, "xh", 1)

    now_keys = swapped(keys[0])
    now_target = swapped(values[0] * rates[0][:, None])
    pieces = [queries[0]] + [
        piece for s in range(1, spans) for piece in (keys[s], values[s] * rates[s][:, None], queries[s])
    ]
    kept, sent = zip(*[sides(piece) for piece in pieces])
    order = owner_order[0]
    later, order, *first_came = lax.optimization_barrier(
        (jnp.stack(sent), order, now_keys[1], now_target[1])
    )
    now_keys, now_target = (now_keys[0], first_came[0]), (now_target[0], first_came[1])
    came = shift(later, "xh", 1)
    other = shift(order, "xh", 1)
    pairs = [(kept[n], came[n]) for n in range(len(kept))]

    weights = [jnp.where(low_side, w[0], w[1]) for w in (w_first, w_second, w_third)]
    eta = jnp.where(low_side, step_size[:1], step_size[1:])
    outputs = []
    chunks = gradients(place, now_keys, now_target, weights)
    for span in range(spans):
        updates = share(orthogonal(place, sum_to_diagonals(place, *chunks)))
        now = pairs[3 * span]
        if span + 1 < spans:
            later = pairs[3 * span + 1], pairs[3 * span + 2]
            weights, *chunks = update_and_gradients(place, eta, *later, updates, weights)
            outputs.append(apply_fast(jnp.concatenate(now), *weights))
        else:
            outputs.append(update_and_apply(place, eta, now, updates, weights))
    results = jnp.concatenate(outputs, axis=0)

    def locate(tokens, block):
        return (tokens // rows) * (2 * rows) + block * rows + tokens % rows

    here, there = locate(order, 0), locate(other, 1)
    low = jnp.where(low_side, here, there).reshape(heads, 1, -1)
    high = jnp.where(low_side, there, here).reshape(heads, 1, -1)
    index = jnp.concatenate([low, high], axis=1).reshape(-1)
    picked = jnp.take(results, index, axis=0)
    regrouped = lax.all_to_all(picked, ("xl", "core", "xh"), split_axis=0, concat_axis=0, tiled=True)
    return finish(regrouped.reshape(2 * heads, -1, size), gate[0], gain[None])[None]


def solution(mesh):
    split = Mesh(
        mesh.devices.reshape([count for _, count in SPLIT]), [name for name, _ in SPLIT]
    )
    in_specs = (
        P(None, CTX, HEAD),
        P(None, CTX, HEAD),
        P(None, CTX, HEAD),
        P(None, CTX),
        P(HEAD, None, None),
        P(HEAD, None, None),
        P(HEAD, None, None),
        P(HEAD),
        P(CTX, None),
        P(CTX, HEAD, None),
        P(),
    )
    out_specs = P(CTX, HEAD, None)
    return jax.shard_map(
        on_device, mesh=split, in_specs=in_specs, out_specs=out_specs, check_vma=False
    )
```

```python
import jax
import jax.numpy as jnp
from jax import lax
from jax.experimental import pallas as pl
from jax.experimental.pallas import tpu as pltpu
from jax.sharding import Mesh, PartitionSpec as P

NS_STEPS = 5
COEFFS = (3.4445, -4.775, 2.0315)
HIGH = lax.Precision.HIGH
SPLIT = (("xl", 2), ("core", 2), ("y", 4), ("xh", 2), ("z", 4))
HEAD = ("xl", "core")
CTX = ("y", "xh", "z")
SIZES = dict(SPLIT)
RING = 4
STEPS = (2, 1, 3)
F32, BF16 = jnp.float32, jnp.bfloat16
VMEM = pl.BlockSpec(memory_space=pltpu.VMEM)
SMEM = pl.BlockSpec(memory_space=pltpu.SMEM)
PARAMS = pltpu.CompilerParams(vmem_limit_bytes=50 * 2**20)


def shift(value, axis, by):
    count = SIZES[axis]
    return lax.ppermute(value, axis, [(i, (i + by) % count) for i in range(count)])


def dot(left, right, spec):
    return jnp.einsum(spec, left, right, precision=HIGH, preferred_element_type=F32)


def halves(value):
    high = value.astype(BF16)
    return high, (value - high.astype(F32)).astype(BF16)


def product(left, right, left_dim=1, right_dim=0):
    def one(a, b):
        return lax.dot_general(
            a, b, (((left_dim,), (right_dim,)), ((), ())), preferred_element_type=F32
        )

    return one(left[0], right[0]) + (one(left[0], right[1]) + one(left[1], right[0]))


def add_gradients(keys, target, w1, w2, w3, grads, before=None):
    keys, target = halves(keys), halves(target)

    def put(m, value):
        grads[m] = value if before is None else before[m] + value

    first = product(keys, halves(w1[...]))
    third = product(keys, halves(w3[...]))
    sigma = jax.nn.sigmoid(first)
    swish = first * sigma
    put(1, product(halves(swish * third), target, 0, 0))
    back = product(target, halves(w2[...]), 1, 1)
    put(2, product(keys, halves(back * swish), 0, 0))
    d_first = back * third * sigma * (1.0 + first * (1.0 - sigma))
    put(0, product(keys, halves(d_first), 0, 0))


def put_chunks(place, grads, tops, lows):
    row = tops[0].shape[1]
    half = row * RING
    for d in range(RING):
        top = pl.multiple_of(((place[0] + d) & (RING - 1)) * row, row)
        low = pl.multiple_of(((place[1] + d) & (RING - 1)) * row + half, row)
        tops[d][...] = grads[:, pl.ds(top, row), :]
        lows[d][...] = grads[:, pl.ds(low, row), :]


def add_updates(place, eta, updates, weights, outs):
    kind = place[0] + place[1]
    for m in range(3):
        for e in range(RING):

            @pl.when(((m - kind) & (RING - 1)) == e)
            def _(m=m, e=e):
                outs[m][...] = weights[m][...] + eta[0] * updates[e][...]


def own_kernel(keys, target, w1, w2, w3, grads):
    add_gradients(keys[...], target[...], w1, w2, w3, grads)


def came_kernel(place, before, keys, target, w1, w2, w3, *rest):
    grads = rest[2 * RING]
    add_gradients(keys[...], target[...], w1, w2, w3, grads, before)
    put_chunks(place, grads, rest[:RING], rest[RING : 2 * RING])


def next_kernel(place, eta, k_own, k_came, t_own, t_came, *refs):
    updates, weights, outs = refs[:RING], refs[4:7], refs[7:10]
    tops, lows, grads = refs[10 : 10 + RING], refs[10 + RING : 10 + 2 * RING], refs[10 + 2 * RING]
    add_updates(place, eta, updates, weights, outs)
    keys = jnp.concatenate([k_own[...], k_came[...]], axis=0)
    target = jnp.concatenate([t_own[...], t_came[...]], axis=0)
    add_gradients(keys, target, *outs, grads)
    put_chunks(place, grads, tops, lows)


def last_kernel(place, eta, q_own, q_came, *refs):
    updates, weights, result, held = refs[:RING], refs[4:7], refs[7], refs[8:]
    add_updates(place, eta, updates, weights, held)
    queries = halves(jnp.concatenate([q_own[...], q_came[...]], axis=0))
    first = product(queries, halves(held[0][...]))
    third = product(queries, halves(held[2][...]))
    result[...] = product(halves(first * jax.nn.sigmoid(first) * third), halves(held[1][...]))


def gradient_cost(rows, size):
    return pl.CostEstimate(
        flops=36 * rows * size * size, bytes_accessed=32 * size * size, transcendentals=rows * size
    )


def gradients(place, keys, target, weights):
    size = weights[0].shape[0]
    chunk = jax.ShapeDtypeStruct((3, size // 2 // RING, size), F32)
    cost = gradient_cost(keys[0].shape[0], size)
    own = pl.pallas_call(
        own_kernel,
        out_shape=jax.ShapeDtypeStruct((3, size, size), F32),
        in_specs=[VMEM] * 5,
        out_specs=VMEM,
        compiler_params=PARAMS,
        cost_estimate=cost,
        name="own_gradients",
    )(keys[0], target[0], *weights)
    out = pl.pallas_call(
        came_kernel,
        out_shape=[chunk] * (2 * RING),
        in_specs=[SMEM] + [VMEM] * 6,
        out_specs=[VMEM] * (2 * RING),
        scratch_shapes=[pltpu.VMEM((3, size, size), F32)],
        compiler_params=PARAMS,
        cost_estimate=cost,
        name="came_gradients",
    )(place, own, keys[1], target[1], *weights)
    return out[:RING], out[RING:]


def update_and_gradients(place, eta, keys, target, updates, weights):
    size = weights[0].shape[0]
    chunk = jax.ShapeDtypeStruct((3, size // 2 // RING, size), F32)
    square = jax.ShapeDtypeStruct((size, size), F32)
    out = pl.pallas_call(
        next_kernel,
        out_shape=[square] * 3 + [chunk] * (2 * RING),
        in_specs=[SMEM, SMEM] + [VMEM] * (RING + 7),
        out_specs=[VMEM] * (3 + 2 * RING),
        scratch_shapes=[pltpu.VMEM((3, size, size), F32)],
        compiler_params=PARAMS,
        cost_estimate=gradient_cost(2 * keys[0].shape[0], size),
        name="update_and_gradients",
    )(place, eta, *keys, *target, *updates, *weights)
    return out[:3], out[3 : 3 + RING], out[3 + RING :]


def update_and_apply(place, eta, queries, updates, weights):
    size = weights[0].shape[0]
    rows = 2 * queries[0].shape[0]
    return pl.pallas_call(
        last_kernel,
        out_shape=jax.ShapeDtypeStruct((rows, size), F32),
        in_specs=[SMEM, SMEM] + [VMEM] * (RING + 5),
        out_specs=VMEM,
        scratch_shapes=[pltpu.VMEM((size, size), F32)] * 3,
        compiler_params=PARAMS,
        cost_estimate=pl.CostEstimate(
            flops=18 * rows * size * size, bytes_accessed=32 * size * size, transcendentals=rows * size
        ),
        name="update_and_apply",
    )(place, eta, *queries, *updates, *weights)


def pick_kernel(place, *refs):
    kind = place[0] + place[1]
    for half in range(2):
        parts, outs = refs[half : 2 * RING : 2], refs[2 * RING + half :: 2]
        for d in range(RING):
            matrix = jnp.minimum((kind + d) & (RING - 1), 2)
            outs[d][...] = parts[0][matrix] + (parts[1][matrix] + (parts[2][matrix] + parts[3][matrix]))


def pick(place, parts):
    chunk = jax.ShapeDtypeStruct(parts[0].shape[1:], F32)
    return pl.pallas_call(
        pick_kernel,
        out_shape=[chunk] * (2 * RING),
        in_specs=[SMEM] + [VMEM] * (2 * RING),
        out_specs=[VMEM] * (2 * RING),
        compiler_params=PARAMS,
        cost_estimate=pl.CostEstimate(
            flops=8 * parts[0].size, bytes_accessed=44 * parts[0].size, transcendentals=0
        ),
        name="pick",
    )(place, *parts)


def hold_kernel(*refs):
    parts, out = refs[: 2 * RING], refs[2 * RING]
    for half in range(2):
        one = [ref[...] for ref in parts[half::2]]
        out[half] = one[0] + (one[1] + (one[2] + one[3]))


def hold(parts):
    return pl.pallas_call(
        hold_kernel,
        out_shape=jax.ShapeDtypeStruct((2,) + parts[0].shape, F32),
        in_specs=[VMEM] * (2 * RING),
        out_specs=VMEM,
        compiler_params=PARAMS,
        cost_estimate=pl.CostEstimate(
            flops=8 * parts[0].size, bytes_accessed=40 * parts[0].size, transcendentals=0
        ),
        name="hold",
    )(*parts)


def orthogonal_kernel(place, *refs):
    chunks, out, (x, exact, xh, xl, ah, al, bh, bl) = refs[:RING], refs[4], refs[5:]
    size = x.shape[0]
    row, half = size // 2 // RING, size // 2
    for d in range(RING):
        top = pl.multiple_of(((place[0] - d) & (RING - 1)) * row, row)
        low = pl.multiple_of(((place[1] + d) & (RING - 1)) * row + half, row)
        x[pl.ds(top, row), :] = chunks[d][0]
        x[pl.ds(low, row), :] = chunks[d][1]
    g = x[...]
    scaled = g / (jnp.sqrt(jnp.sum(g * g)) + 1e-07)
    x[...] = scaled
    xh[...], xl[...] = halves(scaled)

    def part(i):
        return slice(i * half, (i + 1) * half)

    def rows(pair, i):
        return tuple(ref[part(i), :] for ref in pair)

    def symmetric(pair, make):
        for i, j in ((0, 0), (0, 1), (1, 1)):
            value = make(i, j)
            for ref, piece in zip(pair, halves(value)):
                ref[part(i), part(j)] = piece
            if i != j:
                for ref, piece in zip(pair, halves(value.T)):
                    ref[part(j), part(i)] = piece

    xs, squares, blends = (xh, xl), (ah, al), (bh, bl)

    def square(i, j):
        value = product(rows(xs, i), rows(xs, j), 1, 1)
        exact[part(i), part(j)] = value
        return value

    def blend(i, j):
        fourth = product(rows(squares, i), rows(squares, j), 1, 1)
        return COEFFS[1] * exact[part(i), part(j)] + COEFFS[2] * fourth

    for _ in range(NS_STEPS):
        symmetric(squares, square)
        symmetric(blends, blend)
        whole = (xh[...], xl[...])
        news = [COEFFS[0] * x[part(i), :] + product(rows(blends, i), whole) for i in range(2)]
        for i, new in enumerate(news):
            x[part(i), :] = new
            xh[part(i), :], xl[part(i), :] = halves(new)
    out[...] = x[...]


def orthogonal(place, chunks):
    size = chunks[0].shape[-1]
    return pl.pallas_call(
        orthogonal_kernel,
        out_shape=jax.ShapeDtypeStruct((size, size), F32),
        in_specs=[SMEM] + [VMEM] * RING,
        out_specs=VMEM,
        scratch_shapes=[pltpu.VMEM((size, size), F32)] * 2 + [pltpu.VMEM((size, size), BF16)] * 6,
        compiler_params=PARAMS,
        cost_estimate=pl.CostEstimate(
            flops=15 * 6 * size**3, bytes_accessed=8 * size * size, transcendentals=0
        ),
        name="orthogonal",
    )(place, *chunks)


def finish_kernel(picked, gate, gain, out):
    heads, _, size = picked.shape
    total = sum(jnp.sum(picked[h] * picked[h], axis=1, keepdims=True) for h in range(heads))
    scale = lax.rsqrt(total / (heads * size) + 1e-06)
    for h in range(heads):
        here = slice(h * size, (h + 1) * size)
        now = gate[:, here]
        out[:, here] = picked[h] * scale * gain[:, here] * (now * jax.nn.sigmoid(now))


def finish(picked, gate, gain):
    return pl.pallas_call(
        finish_kernel,
        out_shape=jax.ShapeDtypeStruct(gate.shape, F32),
        in_specs=[VMEM] * 3,
        out_specs=VMEM,
        compiler_params=PARAMS,
        cost_estimate=pl.CostEstimate(
            flops=8 * gate.size, bytes_accessed=12 * gate.size, transcendentals=gate.size
        ),
        name="finish",
    )(picked, gate, gain)


def apply_fast(queries, first_w, second_w, third_w):
    first = dot(queries, first_w, "td,de->te")
    third = dot(queries, third_w, "td,de->te")
    return dot(jax.nn.silu(first) * third, second_w, "td,de->te")


def plane_shift(value, dy, dz, used=lambda y, z: True):
    pairs = [
        (y * RING + z, (y + dy) % RING * RING + (z + dz) % RING)
        for y in range(RING)
        for z in range(RING)
        if used(y, z)
    ]
    return lax.ppermute(value, ("y", "z"), pairs)


def sum_to_diagonals(place, tops, lows):
    parts = [tops[0], lows[0]]
    for d in STEPS:
        parts += [plane_shift(tops[d], d, 0), plane_shift(lows[d], 0, d)]
    wanted = pick(place, parts)
    parts = list(wanted[:2])
    for d in STEPS:
        parts += [plane_shift(wanted[2 * d], 0, d), plane_shift(wanted[2 * d + 1], d, 0)]
    held = hold(parts)
    return [held] + [plane_shift(held, d, -d) for d in range(1, RING)]


def share(update):
    used = lambda y, z: (y + z) % RING < 3
    opposite = plane_shift(update, RING // 2, 0, used)
    return [update, plane_shift(update, 0, -1, used), opposite, plane_shift(update, 0, 1, used)]


def on_device(
    keys, values, queries, rates, w_first, w_second, w_third, step_size, owner_order, gate, gain
):
    size = w_first.shape[1]
    spans, rows = keys.shape[0], keys.shape[1]
    mine = lax.axis_index("xh")
    low_side = mine == 0
    heads = SIZES["xl"] * SIZES["core"]
    place = jnp.stack([lax.axis_index("y"), lax.axis_index("z")]).astype(jnp.int32)

    def sides(array):
        left, right = array[:, :size], array[:, size:]
        return jnp.where(low_side, left, right), jnp.where(low_side, right, left)

    kept, sent = sides(keys[0])
    sent, first_values = lax.optimization_barrier((sent, values[0]))
    now_keys = kept, shift(sent, "xh", 1)
    kept, sent = sides(first_values * rates[0][:, None])
    now_target = kept, shift(sent, "xh", 1)
    pieces = [queries[0]] + [
        piece for s in range(1, spans) for piece in (keys[s], values[s] * rates[s][:, None], queries[s])
    ]
    kept, sent = zip(*[sides(piece) for piece in pieces])
    order = owner_order[0]
    row = jnp.zeros((8, size), F32).at[0, : order.shape[0]].set(order.astype(F32))
    later, *first_came = lax.optimization_barrier(
        (jnp.concatenate(sent + (row,)), now_keys[1], now_target[1])
    )
    now_keys, now_target = (now_keys[0], first_came[0]), (now_target[0], first_came[1])
    came = shift(later, "xh", 1)
    other = came[rows * len(kept), : order.shape[0]].astype(jnp.int32)
    pairs = [(kept[n], came[rows * n : rows * (n + 1)]) for n in range(len(kept))]

    weights = [jnp.where(low_side, w[0], w[1]) for w in (w_first, w_second, w_third)]
    eta = jnp.where(low_side, step_size[:1], step_size[1:])
    outputs = []
    chunks = gradients(place, now_keys, now_target, weights)
    for span in range(spans):
        updates = share(orthogonal(place, sum_to_diagonals(place, *chunks)))
        now = pairs[3 * span]
        if span + 1 < spans:
            later = pairs[3 * span + 1], pairs[3 * span + 2]
            weights, *chunks = update_and_gradients(place, eta, *later, updates, weights)
            outputs.append(apply_fast(jnp.concatenate(now), *weights))
        else:
            outputs.append(update_and_apply(place, eta, now, updates, weights))
    results = jnp.concatenate(outputs, axis=0)

    def locate(tokens, block):
        return jnp.where(tokens < rows, tokens, tokens + rows) + block * rows

    here, there = locate(order, 0), locate(other, 1)
    low = jnp.where(low_side, here, there).reshape(heads, 1, -1)
    high = jnp.where(low_side, there, here).reshape(heads, 1, -1)
    index = jnp.concatenate([low, high], axis=1).reshape(-1)
    picked = jnp.take(results, index, axis=0)
    regrouped = lax.all_to_all(picked, ("xl", "core", "xh"), split_axis=0, concat_axis=0, tiled=True)
    return finish(regrouped.reshape(2 * heads, -1, size), gate[0], gain[None])[None]


def solution(mesh):
    split = Mesh(
        mesh.devices.reshape([count for _, count in SPLIT]), [name for name, _ in SPLIT]
    )
    in_specs = (
        P(None, CTX, HEAD),
        P(None, CTX, HEAD),
        P(None, CTX, HEAD),
        P(None, CTX),
        P(HEAD, None, None),
        P(HEAD, None, None),
        P(HEAD, None, None),
        P(HEAD),
        P(CTX, None),
        P(CTX, HEAD, None),
        P(),
    )
    out_specs = P(CTX, HEAD, None)
    return jax.shard_map(
        on_device, mesh=split, in_specs=in_specs, out_specs=out_specs, check_vma=False
    )
```

```python
import jax
import jax.numpy as jnp
from jax import lax
from jax.experimental import pallas as pl
from jax.experimental.pallas import tpu as pltpu
from jax.sharding import Mesh, PartitionSpec as P

NS_STEPS = 5
COEFFS = (3.4445, -4.775, 2.0315)
HIGH = lax.Precision.HIGH
SPLIT = (("xl", 2), ("core", 2), ("y", 4), ("xh", 2), ("z", 4))
HEAD = ("xl", "core")
CTX = ("y", "xh", "z")
SIZES = dict(SPLIT)
RING = 4
STEPS = (2, 1, 3)
F32, BF16 = jnp.float32, jnp.bfloat16
VMEM = pl.BlockSpec(memory_space=pltpu.VMEM)
SMEM = pl.BlockSpec(memory_space=pltpu.SMEM)


def params(mebibytes):
    return pltpu.CompilerParams(vmem_limit_bytes=mebibytes * 2**20)


def shift(value, axis, by):
    count = SIZES[axis]
    return lax.ppermute(value, axis, [(i, (i + by) % count) for i in range(count)])


def dot(left, right, spec):
    return jnp.einsum(spec, left, right, precision=HIGH, preferred_element_type=F32)


def halves(value):
    high = value.astype(BF16)
    return high, (value - high.astype(F32)).astype(BF16)


def product(left, right, left_dim=1, right_dim=0):
    def one(a, b):
        return lax.dot_general(
            a, b, (((left_dim,), (right_dim,)), ((), ())), preferred_element_type=F32
        )

    return one(left[0], right[0]) + (one(left[0], right[1]) + one(left[1], right[0]))


def add_gradients(keys, target, w1, w2, w3, grads, before=None):
    keys, target = halves(keys), halves(target)

    def put(m, value):
        grads[m] = value if before is None else before[m] + value

    first = product(keys, halves(w1[...]))
    third = product(keys, halves(w3[...]))
    sigma = jax.nn.sigmoid(first)
    swish = first * sigma
    put(1, product(halves(swish * third), target, 0, 0))
    back = product(target, halves(w2[...]), 1, 1)
    put(2, product(keys, halves(back * swish), 0, 0))
    d_first = back * third * sigma * (1.0 + first * (1.0 - sigma))
    put(0, product(keys, halves(d_first), 0, 0))


def put_chunks(place, grads, tops, lows):
    row = tops[0].shape[1]
    half = row * RING
    for d in range(RING):
        top = pl.multiple_of(((place[0] + d) & (RING - 1)) * row, row)
        low = pl.multiple_of(((place[1] + d) & (RING - 1)) * row + half, row)
        tops[d][...] = grads[:, pl.ds(top, row), :]
        lows[d][...] = grads[:, pl.ds(low, row), :]


def add_updates(place, eta, updates, weights, outs):
    kind = place[0] + place[1]
    for m in range(3):
        for e in range(RING):

            @pl.when(((m - kind) & (RING - 1)) == e)
            def _(m=m, e=e):
                outs[m][...] = weights[m][...] + eta[0] * updates[e][...]


def own_kernel(keys, target, w1, w2, w3, grads):
    add_gradients(keys[...], target[...], w1, w2, w3, grads)


def came_kernel(place, before, keys, target, w1, w2, w3, *rest):
    grads = rest[2 * RING]
    add_gradients(keys[...], target[...], w1, w2, w3, grads, before)
    put_chunks(place, grads, rest[:RING], rest[RING : 2 * RING])


def next_kernel(place, eta, k_own, k_came, t_own, t_came, *refs):
    updates, weights, outs = refs[:RING], refs[4:7], refs[7:10]
    tops, lows, grads = refs[10 : 10 + RING], refs[10 + RING : 10 + 2 * RING], refs[10 + 2 * RING]
    add_updates(place, eta, updates, weights, outs)
    keys = jnp.concatenate([k_own[...], k_came[...]], axis=0)
    target = jnp.concatenate([t_own[...], t_came[...]], axis=0)
    add_gradients(keys, target, *outs, grads)
    put_chunks(place, grads, tops, lows)


def last_kernel(place, eta, q_own, q_came, *refs):
    updates, weights, result, held = refs[:RING], refs[4:7], refs[7], refs[8:]
    add_updates(place, eta, updates, weights, held)
    queries = halves(jnp.concatenate([q_own[...], q_came[...]], axis=0))
    first = product(queries, halves(held[0][...]))
    third = product(queries, halves(held[2][...]))
    result[...] = product(halves(first * jax.nn.sigmoid(first) * third), halves(held[1][...]))


def gradient_cost(rows, size):
    return pl.CostEstimate(
        flops=36 * rows * size * size, bytes_accessed=32 * size * size, transcendentals=rows * size
    )


def gradients(place, keys, target, weights):
    size = weights[0].shape[0]
    chunk = jax.ShapeDtypeStruct((3, size // 2 // RING, size), F32)
    cost = gradient_cost(keys[0].shape[0], size)
    own = pl.pallas_call(
        own_kernel,
        out_shape=jax.ShapeDtypeStruct((3, size, size), F32),
        in_specs=[VMEM] * 5,
        out_specs=VMEM,
        compiler_params=params(20),
        cost_estimate=cost,
        name="own_gradients",
    )(keys[0], target[0], *weights)
    out = pl.pallas_call(
        came_kernel,
        out_shape=[chunk] * (2 * RING),
        in_specs=[SMEM] + [VMEM] * 6,
        out_specs=[VMEM] * (2 * RING),
        scratch_shapes=[pltpu.VMEM((3, size, size), F32)],
        compiler_params=params(24),
        cost_estimate=cost,
        name="came_gradients",
    )(place, own, keys[1], target[1], *weights)
    return out[:RING], out[RING:]


def update_and_gradients(place, eta, keys, target, updates, weights):
    size = weights[0].shape[0]
    chunk = jax.ShapeDtypeStruct((3, size // 2 // RING, size), F32)
    square = jax.ShapeDtypeStruct((size, size), F32)
    out = pl.pallas_call(
        next_kernel,
        out_shape=[square] * 3 + [chunk] * (2 * RING),
        in_specs=[SMEM, SMEM] + [VMEM] * (RING + 7),
        out_specs=[VMEM] * (3 + 2 * RING),
        scratch_shapes=[pltpu.VMEM((3, size, size), F32)],
        compiler_params=params(30),
        cost_estimate=gradient_cost(2 * keys[0].shape[0], size),
        name="update_and_gradients",
    )(place, eta, *keys, *target, *updates, *weights)
    return out[:3], out[3 : 3 + RING], out[3 + RING :]


def update_and_apply(place, eta, queries, updates, weights):
    size = weights[0].shape[0]
    rows = 2 * queries[0].shape[0]
    return pl.pallas_call(
        last_kernel,
        out_shape=jax.ShapeDtypeStruct((rows, size), F32),
        in_specs=[SMEM, SMEM] + [VMEM] * (RING + 5),
        out_specs=VMEM,
        scratch_shapes=[pltpu.VMEM((size, size), F32)] * 3,
        compiler_params=params(20),
        cost_estimate=pl.CostEstimate(
            flops=18 * rows * size * size, bytes_accessed=32 * size * size, transcendentals=rows * size
        ),
        name="update_and_apply",
    )(place, eta, *queries, *updates, *weights)


def pick_kernel(place, *refs):
    kind = place[0] + place[1]
    for half in range(2):
        parts, outs = refs[half : 2 * RING : 2], refs[2 * RING + half :: 2]
        for d in range(RING):
            matrix = jnp.minimum((kind + d) & (RING - 1), 2)
            outs[d][...] = parts[0][matrix] + (parts[1][matrix] + (parts[2][matrix] + parts[3][matrix]))


def pick(place, parts):
    chunk = jax.ShapeDtypeStruct(parts[0].shape[1:], F32)
    return pl.pallas_call(
        pick_kernel,
        out_shape=[chunk] * (2 * RING),
        in_specs=[SMEM] + [VMEM] * (2 * RING),
        out_specs=[VMEM] * (2 * RING),
        compiler_params=params(6),
        cost_estimate=pl.CostEstimate(
            flops=8 * parts[0].size, bytes_accessed=44 * parts[0].size, transcendentals=0
        ),
        name="pick",
    )(place, *parts)


def hold_kernel(*refs):
    parts, out = refs[: 2 * RING], refs[2 * RING]
    for half in range(2):
        one = [ref[...] for ref in parts[half::2]]
        out[half] = one[0] + (one[1] + (one[2] + one[3]))


def hold(parts):
    return pl.pallas_call(
        hold_kernel,
        out_shape=jax.ShapeDtypeStruct((2,) + parts[0].shape, F32),
        in_specs=[VMEM] * (2 * RING),
        out_specs=VMEM,
        compiler_params=params(4),
        cost_estimate=pl.CostEstimate(
            flops=8 * parts[0].size, bytes_accessed=40 * parts[0].size, transcendentals=0
        ),
        name="hold",
    )(*parts)


def orthogonal_kernel(place, *refs):
    chunks, out, (x, exact, xh, xl, ah, al, bh, bl) = refs[:RING], refs[4], refs[5:]
    size = x.shape[0]
    row, half = size // 2 // RING, size // 2
    for d in range(RING):
        top = pl.multiple_of(((place[0] - d) & (RING - 1)) * row, row)
        low = pl.multiple_of(((place[1] + d) & (RING - 1)) * row + half, row)
        x[pl.ds(top, row), :] = chunks[d][0]
        x[pl.ds(low, row), :] = chunks[d][1]
    g = x[...]
    scaled = g / (jnp.sqrt(jnp.sum(g * g)) + 1e-07)
    x[...] = scaled
    xh[...], xl[...] = halves(scaled)

    def part(i):
        return slice(i * half, (i + 1) * half)

    def rows(pair, i):
        return tuple(ref[part(i), :] for ref in pair)

    def symmetric(pair, make):
        for i, j in ((0, 0), (0, 1), (1, 1)):
            value = make(i, j)
            for ref, piece in zip(pair, halves(value)):
                ref[part(i), part(j)] = piece
            if i != j:
                for ref, piece in zip(pair, halves(value.T)):
                    ref[part(j), part(i)] = piece

    xs, squares, blends = (xh, xl), (ah, al), (bh, bl)

    def square(i, j):
        value = product(rows(xs, i), rows(xs, j), 1, 1)
        exact[part(i), part(j)] = value
        return value

    def blend(i, j):
        fourth = product(rows(squares, i), rows(squares, j), 1, 1)
        return COEFFS[1] * exact[part(i), part(j)] + COEFFS[2] * fourth

    for _ in range(NS_STEPS):
        symmetric(squares, square)
        symmetric(blends, blend)
        whole = (xh[...], xl[...])
        news = [COEFFS[0] * x[part(i), :] + product(rows(blends, i), whole) for i in range(2)]
        for i, new in enumerate(news):
            x[part(i), :] = new
            xh[part(i), :], xl[part(i), :] = halves(new)
    out[...] = x[...]


def orthogonal(place, chunks):
    size = chunks[0].shape[-1]
    return pl.pallas_call(
        orthogonal_kernel,
        out_shape=jax.ShapeDtypeStruct((size, size), F32),
        in_specs=[SMEM] + [VMEM] * RING,
        out_specs=VMEM,
        scratch_shapes=[pltpu.VMEM((size, size), F32)] * 2 + [pltpu.VMEM((size, size), BF16)] * 6,
        compiler_params=params(14),
        cost_estimate=pl.CostEstimate(
            flops=15 * 6 * size**3, bytes_accessed=8 * size * size, transcendentals=0
        ),
        name="orthogonal",
    )(place, *chunks)


def finish_kernel(picked, gate, gain, out):
    heads, _, size = picked.shape
    total = sum(jnp.sum(picked[h] * picked[h], axis=1, keepdims=True) for h in range(heads))
    scale = lax.rsqrt(total / (heads * size) + 1e-06)
    for h in range(heads):
        here = slice(h * size, (h + 1) * size)
        now = gate[:, here]
        out[:, here] = picked[h] * scale * gain[:, here] * (now * jax.nn.sigmoid(now))


def finish(picked, gate, gain):
    return pl.pallas_call(
        finish_kernel,
        out_shape=jax.ShapeDtypeStruct(gate.shape, F32),
        in_specs=[VMEM] * 3,
        out_specs=VMEM,
        compiler_params=params(10),
        cost_estimate=pl.CostEstimate(
            flops=8 * gate.size, bytes_accessed=12 * gate.size, transcendentals=gate.size
        ),
        name="finish",
    )(picked, gate, gain)


def apply_fast(queries, first_w, second_w, third_w):
    first = dot(queries, first_w, "td,de->te")
    third = dot(queries, third_w, "td,de->te")
    return dot(jax.nn.silu(first) * third, second_w, "td,de->te")


def plane_shift(value, dy, dz, used=lambda y, z: True):
    pairs = [
        (y * RING + z, (y + dy) % RING * RING + (z + dz) % RING)
        for y in range(RING)
        for z in range(RING)
        if used(y, z)
    ]
    return lax.ppermute(value, ("y", "z"), pairs)


def sum_to_diagonals(place, tops, lows):
    parts = [tops[0], lows[0]]
    for d in STEPS:
        parts += [plane_shift(tops[d], d, 0), plane_shift(lows[d], 0, d)]
    wanted = pick(place, parts)
    parts = list(wanted[:2])
    for d in STEPS:
        parts += [plane_shift(wanted[2 * d], 0, d), plane_shift(wanted[2 * d + 1], d, 0)]
    held = hold(parts)
    return [held] + [plane_shift(held, d, -d) for d in range(1, RING)]


def share(update):
    used = lambda y, z: (y + z) % RING < 3
    opposite = plane_shift(update, RING // 2, 0, used)
    return [update, plane_shift(update, 0, -1, used), opposite, plane_shift(update, 0, 1, used)]


def on_device(
    keys, values, queries, rates, w_first, w_second, w_third, step_size, owner_order, gate, gain
):
    size = w_first.shape[1]
    spans, rows = keys.shape[0], keys.shape[1]
    mine = lax.axis_index("xh")
    low_side = mine == 0
    heads = SIZES["xl"] * SIZES["core"]
    place = jnp.stack([lax.axis_index("y"), lax.axis_index("z")]).astype(jnp.int32)

    def sides(array):
        left, right = array[:, :size], array[:, size:]
        return jnp.where(low_side, left, right), jnp.where(low_side, right, left)

    kept, sent = sides(keys[0])
    sent, first_values = lax.optimization_barrier((sent, values[0]))
    now_keys = kept, shift(sent, "xh", 1)
    kept, sent = sides(first_values * rates[0][:, None])
    now_target = kept, shift(sent, "xh", 1)
    pieces = [queries[0]] + [
        piece for s in range(1, spans) for piece in (keys[s], values[s] * rates[s][:, None], queries[s])
    ]
    kept, sent = zip(*[sides(piece) for piece in pieces])
    order = owner_order[0]
    row = jnp.zeros((8, size), F32).at[0, : order.shape[0]].set(order.astype(F32))
    later, *first_came = lax.optimization_barrier(
        (jnp.concatenate(sent + (row,)), now_keys[1], now_target[1])
    )
    now_keys, now_target = (now_keys[0], first_came[0]), (now_target[0], first_came[1])
    came = shift(later, "xh", 1)
    other = came[rows * len(kept), : order.shape[0]].astype(jnp.int32)
    pairs = [(kept[n], came[rows * n : rows * (n + 1)]) for n in range(len(kept))]

    weights = [jnp.where(low_side, w[0], w[1]) for w in (w_first, w_second, w_third)]
    eta = jnp.where(low_side, step_size[:1], step_size[1:])
    outputs = []
    chunks = gradients(place, now_keys, now_target, weights)
    for span in range(spans):
        updates = share(orthogonal(place, sum_to_diagonals(place, *chunks)))
        now = pairs[3 * span]
        if span + 1 < spans:
            later = pairs[3 * span + 1], pairs[3 * span + 2]
            weights, *chunks = update_and_gradients(place, eta, *later, updates, weights)
            outputs.append(apply_fast(jnp.concatenate(now), *weights))
        else:
            outputs.append(update_and_apply(place, eta, now, updates, weights))
    results = jnp.concatenate(outputs, axis=0)

    def locate(tokens, block):
        return jnp.where(tokens < rows, tokens, tokens + rows) + block * rows

    here, there = locate(order, 0), locate(other, 1)
    low = jnp.where(low_side, here, there).reshape(heads, 1, -1)
    high = jnp.where(low_side, there, here).reshape(heads, 1, -1)
    index = jnp.concatenate([low, high], axis=1).reshape(-1)
    picked = jnp.take(results, index, axis=0)
    regrouped = lax.all_to_all(picked, ("xl", "core", "xh"), split_axis=0, concat_axis=0, tiled=True)
    return finish(regrouped.reshape(2 * heads, -1, size), gate[0], gain[None])[None]


def solution(mesh):
    split = Mesh(
        mesh.devices.reshape([count for _, count in SPLIT]), [name for name, _ in SPLIT]
    )
    in_specs = (
        P(None, CTX, HEAD),
        P(None, CTX, HEAD),
        P(None, CTX, HEAD),
        P(None, CTX),
        P(HEAD, None, None),
        P(HEAD, None, None),
        P(HEAD, None, None),
        P(HEAD),
        P(CTX, None),
        P(CTX, HEAD, None),
        P(),
    )
    out_specs = P(CTX, HEAD, None)
    return jax.shard_map(
        on_device, mesh=split, in_specs=in_specs, out_specs=out_specs, check_vma=False
    )
```

```python
import jax
import jax.numpy as jnp
from jax import lax
from jax.experimental import pallas as pl
from jax.experimental.pallas import tpu as pltpu
from jax.sharding import Mesh, PartitionSpec as P

NS_STEPS = 5
COEFFS = (3.4445, -4.775, 2.0315)
HIGH = lax.Precision.HIGH
SPLIT = (("xl", 2), ("core", 2), ("y", 4), ("xh", 2), ("z", 4))
HEAD = ("xl", "core")
CTX = ("y", "xh", "z")
SIZES = dict(SPLIT)
RING = 4
STEPS = (2, 1, 3)
F32, BF16 = jnp.float32, jnp.bfloat16
VMEM = pl.BlockSpec(memory_space=pltpu.VMEM)
SMEM = pl.BlockSpec(memory_space=pltpu.SMEM)


def params(mebibytes):
    return pltpu.CompilerParams(vmem_limit_bytes=mebibytes * 2**20)


def shift(value, axis, by):
    count = SIZES[axis]
    return lax.ppermute(value, axis, [(i, (i + by) % count) for i in range(count)])


def dot(left, right, spec):
    return jnp.einsum(spec, left, right, precision=HIGH, preferred_element_type=F32)


def halves(value):
    high = value.astype(BF16)
    return high, (value - high.astype(F32)).astype(BF16)


def product(left, right, left_dim=1, right_dim=0):
    def one(a, b):
        return lax.dot_general(
            a, b, (((left_dim,), (right_dim,)), ((), ())), preferred_element_type=F32
        )

    return one(left[0], right[0]) + (one(left[0], right[1]) + one(left[1], right[0]))


def add_gradients(keys, target, w1, w2, w3, grads, before=None):
    keys, target = halves(keys), halves(target)

    def put(m, value):
        grads[m] = value if before is None else before[m] + value

    first = product(keys, halves(w1[...]))
    third = product(keys, halves(w3[...]))
    sigma = jax.nn.sigmoid(first)
    swish = first * sigma
    put(1, product(halves(swish * third), target, 0, 0))
    back = product(target, halves(w2[...]), 1, 1)
    put(2, product(keys, halves(back * swish), 0, 0))
    d_first = back * third * sigma * (1.0 + first * (1.0 - sigma))
    put(0, product(keys, halves(d_first), 0, 0))


def put_chunks(place, grads, tops, lows):
    row = tops[0].shape[1]
    half = row * RING
    for d in range(RING):
        top = pl.multiple_of(((place[0] + d) & (RING - 1)) * row, row)
        low = pl.multiple_of(((place[1] + d) & (RING - 1)) * row + half, row)
        tops[d][...] = grads[:, pl.ds(top, row), :]
        lows[d][...] = grads[:, pl.ds(low, row), :]


def add_updates(place, eta, updates, weights, outs):
    kind = place[0] + place[1]
    for m in range(3):
        for e in range(RING):

            @pl.when(((m - kind) & (RING - 1)) == e)
            def _(m=m, e=e):
                outs[m][...] = weights[m][...] + eta[0] * updates[e][...]


def own_kernel(keys, target, w1, w2, w3, grads):
    add_gradients(keys[...], target[...], w1, w2, w3, grads)


def came_kernel(place, before, keys, target, w1, w2, w3, *rest):
    grads = rest[2 * RING]
    add_gradients(keys[...], target[...], w1, w2, w3, grads, before)
    put_chunks(place, grads, rest[:RING], rest[RING : 2 * RING])


def next_kernel(place, eta, k_own, k_came, t_own, t_came, *refs):
    updates, weights, outs = refs[:RING], refs[4:7], refs[7:10]
    tops, lows, grads = refs[10 : 10 + RING], refs[10 + RING : 10 + 2 * RING], refs[10 + 2 * RING]
    add_updates(place, eta, updates, weights, outs)
    keys = jnp.concatenate([k_own[...], k_came[...]], axis=0)
    target = jnp.concatenate([t_own[...], t_came[...]], axis=0)
    add_gradients(keys, target, *outs, grads)
    put_chunks(place, grads, tops, lows)


def last_kernel(place, eta, q_own, q_came, *refs):
    updates, weights, result, held = refs[:RING], refs[4:7], refs[7], refs[8:]
    add_updates(place, eta, updates, weights, held)
    queries = halves(jnp.concatenate([q_own[...], q_came[...]], axis=0))
    first = product(queries, halves(held[0][...]))
    third = product(queries, halves(held[2][...]))
    result[...] = product(halves(first * jax.nn.sigmoid(first) * third), halves(held[1][...]))


def gradient_cost(rows, size):
    return pl.CostEstimate(
        flops=36 * rows * size * size, bytes_accessed=32 * size * size, transcendentals=rows * size
    )


def gradients(place, keys, target, weights):
    size = weights[0].shape[0]
    chunk = jax.ShapeDtypeStruct((3, size // 2 // RING, size), F32)
    cost = gradient_cost(keys[0].shape[0], size)
    own = pl.pallas_call(
        own_kernel,
        out_shape=jax.ShapeDtypeStruct((3, size, size), F32),
        in_specs=[VMEM] * 5,
        out_specs=VMEM,
        compiler_params=params(20),
        cost_estimate=cost,
        name="own_gradients",
    )(keys[0], target[0], *weights)
    out = pl.pallas_call(
        came_kernel,
        out_shape=[chunk] * (2 * RING),
        in_specs=[SMEM] + [VMEM] * 6,
        out_specs=[VMEM] * (2 * RING),
        scratch_shapes=[pltpu.VMEM((3, size, size), F32)],
        compiler_params=params(24),
        cost_estimate=cost,
        name="came_gradients",
    )(place, own, keys[1], target[1], *weights)
    return out[:RING], out[RING:]


def update_and_gradients(place, eta, keys, target, updates, weights):
    size = weights[0].shape[0]
    chunk = jax.ShapeDtypeStruct((3, size // 2 // RING, size), F32)
    square = jax.ShapeDtypeStruct((size, size), F32)
    out = pl.pallas_call(
        next_kernel,
        out_shape=[square] * 3 + [chunk] * (2 * RING),
        in_specs=[SMEM, SMEM] + [VMEM] * (RING + 7),
        out_specs=[VMEM] * (3 + 2 * RING),
        scratch_shapes=[pltpu.VMEM((3, size, size), F32)],
        compiler_params=params(30),
        cost_estimate=gradient_cost(2 * keys[0].shape[0], size),
        name="update_and_gradients",
    )(place, eta, *keys, *target, *updates, *weights)
    return out[:3], out[3 : 3 + RING], out[3 + RING :]


def update_and_apply(place, eta, queries, updates, weights):
    size = weights[0].shape[0]
    rows = 2 * queries[0].shape[0]
    return pl.pallas_call(
        last_kernel,
        out_shape=jax.ShapeDtypeStruct((rows, size), F32),
        in_specs=[SMEM, SMEM] + [VMEM] * (RING + 5),
        out_specs=VMEM,
        scratch_shapes=[pltpu.VMEM((size, size), F32)] * 3,
        compiler_params=params(20),
        cost_estimate=pl.CostEstimate(
            flops=18 * rows * size * size, bytes_accessed=32 * size * size, transcendentals=rows * size
        ),
        name="update_and_apply",
    )(place, eta, *queries, *updates, *weights)


def pick_kernel(place, *refs):
    kind = place[0] + place[1]
    for half in range(2):
        parts, outs = refs[half : 2 * RING : 2], refs[2 * RING + half :: 2]
        for d in range(RING):
            matrix = jnp.minimum((kind + d) & (RING - 1), 2)
            outs[d][...] = parts[0][matrix] + (parts[1][matrix] + (parts[2][matrix] + parts[3][matrix]))


def pick(place, parts):
    chunk = jax.ShapeDtypeStruct(parts[0].shape[1:], F32)
    return pl.pallas_call(
        pick_kernel,
        out_shape=[chunk] * (2 * RING),
        in_specs=[SMEM] + [VMEM] * (2 * RING),
        out_specs=[VMEM] * (2 * RING),
        compiler_params=params(6),
        cost_estimate=pl.CostEstimate(
            flops=8 * parts[0].size, bytes_accessed=44 * parts[0].size, transcendentals=0
        ),
        name="pick",
    )(place, *parts)


def hold_kernel(*refs):
    parts, out = refs[: 2 * RING], refs[2 * RING]
    for half in range(2):
        one = [ref[...] for ref in parts[half::2]]
        out[half] = one[0] + (one[1] + (one[2] + one[3]))


def hold(parts):
    return pl.pallas_call(
        hold_kernel,
        out_shape=jax.ShapeDtypeStruct((2,) + parts[0].shape, F32),
        in_specs=[VMEM] * (2 * RING),
        out_specs=VMEM,
        compiler_params=params(4),
        cost_estimate=pl.CostEstimate(
            flops=8 * parts[0].size, bytes_accessed=40 * parts[0].size, transcendentals=0
        ),
        name="hold",
    )(*parts)


def orthogonal_kernel(place, *refs):
    chunks, out, (x, exact, xh, xl, ah, al, bh, bl) = refs[:RING], refs[4], refs[5:]
    size = x.shape[0]
    row, half = size // 2 // RING, size // 2
    for d in range(RING):
        top = pl.multiple_of(((place[0] - d) & (RING - 1)) * row, row)
        low = pl.multiple_of(((place[1] + d) & (RING - 1)) * row + half, row)
        x[pl.ds(top, row), :] = chunks[d][0]
        x[pl.ds(low, row), :] = chunks[d][1]
    g = x[...]
    scaled = g / (jnp.sqrt(jnp.sum(g * g)) + 1e-07)
    x[...] = scaled
    xh[...], xl[...] = halves(scaled)

    def part(i):
        return slice(i * half, (i + 1) * half)

    def rows(pair, i):
        return tuple(ref[part(i), :] for ref in pair)

    def symmetric(pair, make):
        for i, j in ((0, 0), (0, 1), (1, 1)):
            value = make(i, j)
            for ref, piece in zip(pair, halves(value)):
                ref[part(i), part(j)] = piece
            if i != j:
                for ref, piece in zip(pair, halves(value.T)):
                    ref[part(j), part(i)] = piece

    xs, squares, blends = (xh, xl), (ah, al), (bh, bl)

    def square(i, j):
        value = product(rows(xs, i), rows(xs, j), 1, 1)
        exact[part(i), part(j)] = value
        return value

    def blend(i, j):
        fourth = product(rows(squares, i), rows(squares, j), 1, 1)
        return COEFFS[1] * exact[part(i), part(j)] + COEFFS[2] * fourth

    for _ in range(NS_STEPS):
        symmetric(squares, square)
        symmetric(blends, blend)
        whole = (xh[...], xl[...])
        news = [COEFFS[0] * x[part(i), :] + product(rows(blends, i), whole) for i in range(2)]
        for i, new in enumerate(news):
            x[part(i), :] = new
            xh[part(i), :], xl[part(i), :] = halves(new)
    out[...] = x[...]


def orthogonal(place, chunks):
    size = chunks[0].shape[-1]
    return pl.pallas_call(
        orthogonal_kernel,
        out_shape=jax.ShapeDtypeStruct((size, size), F32),
        in_specs=[SMEM] + [VMEM] * RING,
        out_specs=VMEM,
        scratch_shapes=[pltpu.VMEM((size, size), F32)] * 2 + [pltpu.VMEM((size, size), BF16)] * 6,
        compiler_params=params(14),
        cost_estimate=pl.CostEstimate(
            flops=15 * 6 * size**3, bytes_accessed=8 * size * size, transcendentals=0
        ),
        name="orthogonal",
    )(place, *chunks)


def finish_kernel(picked, gate, gain, out):
    heads, _, size = picked.shape
    total = sum(jnp.sum(picked[h] * picked[h], axis=1, keepdims=True) for h in range(heads))
    scale = lax.rsqrt(total / (heads * size) + 1e-06)
    for h in range(heads):
        here = slice(h * size, (h + 1) * size)
        now = gate[:, here]
        out[:, here] = picked[h] * scale * gain[:, here] * (now * jax.nn.sigmoid(now))


def finish(picked, gate, gain):
    return pl.pallas_call(
        finish_kernel,
        out_shape=jax.ShapeDtypeStruct(gate.shape, F32),
        in_specs=[VMEM] * 3,
        out_specs=VMEM,
        compiler_params=params(10),
        cost_estimate=pl.CostEstimate(
            flops=8 * gate.size, bytes_accessed=12 * gate.size, transcendentals=gate.size
        ),
        name="finish",
    )(picked, gate, gain)


def apply_fast(queries, first_w, second_w, third_w):
    first = dot(queries, first_w, "td,de->te")
    third = dot(queries, third_w, "td,de->te")
    return dot(jax.nn.silu(first) * third, second_w, "td,de->te")


def plane_shift(value, dy, dz):
    pairs = [
        (y * RING + z, (y + dy) % RING * RING + (z + dz) % RING)
        for y in range(RING)
        for z in range(RING)
    ]
    return lax.ppermute(value, ("y", "z"), pairs)


def sum_to_diagonals(place, tops, lows):
    parts = [tops[0], lows[0]]
    for d in STEPS:
        parts += [plane_shift(tops[d], d, 0), plane_shift(lows[d], 0, d)]
    wanted = pick(place, parts)
    parts = list(wanted[:2])
    for d in STEPS:
        parts += [plane_shift(wanted[2 * d], 0, d), plane_shift(wanted[2 * d + 1], d, 0)]
    held = hold(parts)
    return [held] + [plane_shift(held, d, -d) for d in range(1, RING)]


def share(update):
    opposite = plane_shift(update, RING // 2, 0)
    return [update, plane_shift(update, 0, -1), opposite, plane_shift(update, 0, 1)]


def on_device(
    keys, values, queries, rates, w_first, w_second, w_third, step_size, owner_order, gate, gain
):
    size = w_first.shape[1]
    spans, rows = keys.shape[0], keys.shape[1]
    mine = lax.axis_index("xh")
    low_side = mine == 0
    heads = SIZES["xl"] * SIZES["core"]
    place = jnp.stack([lax.axis_index("y"), lax.axis_index("z")]).astype(jnp.int32)

    def sides(array):
        left, right = array[:, :size], array[:, size:]
        return jnp.where(low_side, left, right), jnp.where(low_side, right, left)

    kept, sent = sides(keys[0])
    sent, first_values = lax.optimization_barrier((sent, values[0]))
    now_keys = kept, shift(sent, "xh", 1)
    kept, sent = sides(first_values * rates[0][:, None])
    now_target = kept, shift(sent, "xh", 1)
    pieces = [queries[0]] + [
        piece for s in range(1, spans) for piece in (keys[s], values[s] * rates[s][:, None], queries[s])
    ]
    kept, sent = zip(*[sides(piece) for piece in pieces])
    order = owner_order[0]
    row = jnp.zeros((8, size), F32).at[0, : order.shape[0]].set(order.astype(F32))
    later, *first_came = lax.optimization_barrier(
        (jnp.concatenate(sent + (row,)), now_keys[1], now_target[1])
    )
    now_keys, now_target = (now_keys[0], first_came[0]), (now_target[0], first_came[1])
    came = shift(later, "xh", 1)
    other = came[rows * len(kept), : order.shape[0]].astype(jnp.int32)
    pairs = [(kept[n], came[rows * n : rows * (n + 1)]) for n in range(len(kept))]

    weights = [jnp.where(low_side, w[0], w[1]) for w in (w_first, w_second, w_third)]
    eta = jnp.where(low_side, step_size[:1], step_size[1:])
    outputs = []
    chunks = gradients(place, now_keys, now_target, weights)
    for span in range(spans):
        updates = share(orthogonal(place, sum_to_diagonals(place, *chunks)))
        now = pairs[3 * span]
        if span + 1 < spans:
            later = pairs[3 * span + 1], pairs[3 * span + 2]
            weights, *chunks = update_and_gradients(place, eta, *later, updates, weights)
            outputs.append(apply_fast(jnp.concatenate(now), *weights))
        else:
            outputs.append(update_and_apply(place, eta, now, updates, weights))
    results = jnp.concatenate(outputs, axis=0)

    def locate(tokens, block):
        return jnp.where(tokens < rows, tokens, tokens + rows) + block * rows

    here, there = locate(order, 0), locate(other, 1)
    low = jnp.where(low_side, here, there).reshape(heads, 1, -1)
    high = jnp.where(low_side, there, here).reshape(heads, 1, -1)
    index = jnp.concatenate([low, high], axis=1).reshape(-1)
    picked = jnp.take(results, index, axis=0)
    regrouped = lax.all_to_all(picked, ("xl", "core", "xh"), split_axis=0, concat_axis=0, tiled=True)
    return finish(regrouped.reshape(2 * heads, -1, size), gate[0], gain[None])[None]


def solution(mesh):
    split = Mesh(
        mesh.devices.reshape([count for _, count in SPLIT]), [name for name, _ in SPLIT]
    )
    in_specs = (
        P(None, CTX, HEAD),
        P(None, CTX, HEAD),
        P(None, CTX, HEAD),
        P(None, CTX),
        P(HEAD, None, None),
        P(HEAD, None, None),
        P(HEAD, None, None),
        P(HEAD),
        P(CTX, None),
        P(CTX, HEAD, None),
        P(),
    )
    out_specs = P(CTX, HEAD, None)
    return jax.shard_map(
        on_device, mesh=split, in_specs=in_specs, out_specs=out_specs, check_vma=False
    )
```

```python
import jax
import jax.numpy as jnp
from jax import lax
from jax.experimental import pallas as pl
from jax.experimental.pallas import tpu as pltpu
from jax.sharding import Mesh, PartitionSpec as P

NS_STEPS = 5
COEFFS = (3.4445, -4.775, 2.0315)
SPLIT = (("xl", 2), ("core", 2), ("y", 4), ("xh", 2), ("z", 4))
HEAD = ("xl", "core")
CTX = ("y", "xh", "z")
SIZES = dict(SPLIT)
RING = 4
STEPS = (2, 1, 3)
F32, BF16 = jnp.float32, jnp.bfloat16
VMEM = pl.BlockSpec(memory_space=pltpu.VMEM)
SMEM = pl.BlockSpec(memory_space=pltpu.SMEM)


def params(mebibytes):
    return pltpu.CompilerParams(vmem_limit_bytes=mebibytes * 2**20)


def shift(value, axis, by):
    count = SIZES[axis]
    return lax.ppermute(value, axis, [(i, (i + by) % count) for i in range(count)])


def halves(value):
    high = value.astype(BF16)
    return high, (value - high.astype(F32)).astype(BF16)


def product(left, right, left_dim=1, right_dim=0):
    def one(a, b):
        return lax.dot_general(
            a, b, (((left_dim,), (right_dim,)), ((), ())), preferred_element_type=F32
        )

    return one(left[0], right[0]) + (one(left[0], right[1]) + one(left[1], right[0]))


def add_gradients(keys, target, w1, w2, w3, grads, before=None):
    keys, target = halves(keys), halves(target)

    def put(m, value):
        grads[m] = value if before is None else before[m] + value

    first = product(keys, halves(w1[...]))
    third = product(keys, halves(w3[...]))
    sigma = jax.nn.sigmoid(first)
    swish = first * sigma
    put(1, product(halves(swish * third), target, 0, 0))
    back = product(target, halves(w2[...]), 1, 1)
    put(2, product(keys, halves(back * swish), 0, 0))
    d_first = back * third * sigma * (1.0 + first * (1.0 - sigma))
    put(0, product(keys, halves(d_first), 0, 0))


def put_chunks(place, grads, tops, lows):
    row = tops[0].shape[1]
    half = row * RING
    for d in range(RING):
        top = pl.multiple_of(((place[0] + d) & (RING - 1)) * row, row)
        low = pl.multiple_of(((place[1] + d) & (RING - 1)) * row + half, row)
        tops[d][...] = grads[:, pl.ds(top, row), :]
        lows[d][...] = grads[:, pl.ds(low, row), :]


def add_updates(place, eta, updates, weights, outs):
    kind = place[0] + place[1]
    for m in range(3):
        for e in range(RING):

            @pl.when(((m - kind) & (RING - 1)) == e)
            def _(m=m, e=e):
                outs[m][...] = weights[m][...] + eta[0] * updates[e][...]


def own_kernel(keys, target, w1, w2, w3, grads):
    add_gradients(keys[...], target[...], w1, w2, w3, grads)


def came_kernel(place, before, keys, target, w1, w2, w3, *rest):
    grads = rest[2 * RING]
    add_gradients(keys[...], target[...], w1, w2, w3, grads, before)
    put_chunks(place, grads, rest[:RING], rest[RING : 2 * RING])


def next_kernel(place, eta, k_own, k_came, t_own, t_came, *refs):
    updates, weights, outs = refs[:RING], refs[4:7], refs[7:10]
    tops, lows, grads = refs[10 : 10 + RING], refs[10 + RING : 10 + 2 * RING], refs[10 + 2 * RING]
    add_updates(place, eta, updates, weights, outs)
    keys = jnp.concatenate([k_own[...], k_came[...]], axis=0)
    target = jnp.concatenate([t_own[...], t_came[...]], axis=0)
    add_gradients(keys, target, *outs, grads)
    put_chunks(place, grads, tops, lows)


def last_kernel(place, eta, q_own, q_came, *refs):
    updates, weights, result, held = refs[:RING], refs[4:7], refs[7], refs[8:]
    add_updates(place, eta, updates, weights, held)
    queries = halves(jnp.concatenate([q_own[...], q_came[...]], axis=0))
    first = product(queries, halves(held[0][...]))
    third = product(queries, halves(held[2][...]))
    result[...] = product(halves(first * jax.nn.sigmoid(first) * third), halves(held[1][...]))


def gradient_cost(rows, size):
    return pl.CostEstimate(
        flops=36 * rows * size * size, bytes_accessed=32 * size * size, transcendentals=rows * size
    )


def gradients(place, keys, target, weights):
    size = weights[0].shape[0]
    chunk = jax.ShapeDtypeStruct((3, size // 2 // RING, size), F32)
    cost = gradient_cost(keys[0].shape[0], size)
    own = pl.pallas_call(
        own_kernel,
        out_shape=jax.ShapeDtypeStruct((3, size, size), F32),
        in_specs=[VMEM] * 5,
        out_specs=VMEM,
        compiler_params=params(20),
        cost_estimate=cost,
        name="own_gradients",
    )(keys[0], target[0], *weights)
    out = pl.pallas_call(
        came_kernel,
        out_shape=[chunk] * (2 * RING),
        in_specs=[SMEM] + [VMEM] * 6,
        out_specs=[VMEM] * (2 * RING),
        scratch_shapes=[pltpu.VMEM((3, size, size), F32)],
        compiler_params=params(24),
        cost_estimate=cost,
        name="came_gradients",
    )(place, own, keys[1], target[1], *weights)
    return out[:RING], out[RING:]


def update_and_gradients(place, eta, keys, target, updates, weights):
    size = weights[0].shape[0]
    chunk = jax.ShapeDtypeStruct((3, size // 2 // RING, size), F32)
    square = jax.ShapeDtypeStruct((size, size), F32)
    out = pl.pallas_call(
        next_kernel,
        out_shape=[square] * 3 + [chunk] * (2 * RING),
        in_specs=[SMEM, SMEM] + [VMEM] * (RING + 7),
        out_specs=[VMEM] * (3 + 2 * RING),
        scratch_shapes=[pltpu.VMEM((3, size, size), F32)],
        compiler_params=params(30),
        cost_estimate=gradient_cost(2 * keys[0].shape[0], size),
        name="update_and_gradients",
    )(place, eta, *keys, *target, *updates, *weights)
    return out[:3], out[3 : 3 + RING], out[3 + RING :]


def update_and_apply(place, eta, queries, updates, weights):
    size = weights[0].shape[0]
    rows = 2 * queries[0].shape[0]
    return pl.pallas_call(
        last_kernel,
        out_shape=jax.ShapeDtypeStruct((rows, size), F32),
        in_specs=[SMEM, SMEM] + [VMEM] * (RING + 5),
        out_specs=VMEM,
        scratch_shapes=[pltpu.VMEM((size, size), F32)] * 3,
        compiler_params=params(20),
        cost_estimate=pl.CostEstimate(
            flops=18 * rows * size * size, bytes_accessed=32 * size * size, transcendentals=rows * size
        ),
        name="update_and_apply",
    )(place, eta, *queries, *updates, *weights)


def pick_kernel(place, *refs):
    kind = place[0] + place[1]
    for half in range(2):
        parts, outs = refs[half : 2 * RING : 2], refs[2 * RING + half :: 2]
        for d in range(RING):
            matrix = jnp.minimum((kind + d) & (RING - 1), 2)
            outs[d][...] = parts[0][matrix] + (parts[1][matrix] + (parts[2][matrix] + parts[3][matrix]))


def pick(place, parts):
    chunk = jax.ShapeDtypeStruct(parts[0].shape[1:], F32)
    return pl.pallas_call(
        pick_kernel,
        out_shape=[chunk] * (2 * RING),
        in_specs=[SMEM] + [VMEM] * (2 * RING),
        out_specs=[VMEM] * (2 * RING),
        compiler_params=params(6),
        cost_estimate=pl.CostEstimate(
            flops=8 * parts[0].size, bytes_accessed=44 * parts[0].size, transcendentals=0
        ),
        name="pick",
    )(place, *parts)


def hold_kernel(*refs):
    parts, out = refs[: 2 * RING], refs[2 * RING]
    for half in range(2):
        one = [ref[...] for ref in parts[half::2]]
        out[half] = one[0] + (one[1] + (one[2] + one[3]))


def hold(parts):
    return pl.pallas_call(
        hold_kernel,
        out_shape=jax.ShapeDtypeStruct((2,) + parts[0].shape, F32),
        in_specs=[VMEM] * (2 * RING),
        out_specs=VMEM,
        compiler_params=params(4),
        cost_estimate=pl.CostEstimate(
            flops=8 * parts[0].size, bytes_accessed=40 * parts[0].size, transcendentals=0
        ),
        name="hold",
    )(*parts)


def orthogonal_kernel(place, *refs):
    chunks, out, (x, exact, xh, xl, ah, al, bh, bl) = refs[:RING], refs[4], refs[5:]
    size = x.shape[0]
    row, half = size // 2 // RING, size // 2
    for d in range(RING):
        top = pl.multiple_of(((place[0] - d) & (RING - 1)) * row, row)
        low = pl.multiple_of(((place[1] + d) & (RING - 1)) * row + half, row)
        x[pl.ds(top, row), :] = chunks[d][0]
        x[pl.ds(low, row), :] = chunks[d][1]
    g = x[...]
    scaled = g / (jnp.sqrt(jnp.sum(g * g)) + 1e-07)
    x[...] = scaled
    xh[...], xl[...] = halves(scaled)

    def part(i):
        return slice(i * half, (i + 1) * half)

    def rows(pair, i):
        return tuple(ref[part(i), :] for ref in pair)

    def symmetric(pair, make):
        for i, j in ((0, 0), (0, 1), (1, 1)):
            value = make(i, j)
            for ref, piece in zip(pair, halves(value)):
                ref[part(i), part(j)] = piece
            if i != j:
                for ref, piece in zip(pair, halves(value.T)):
                    ref[part(j), part(i)] = piece

    xs, squares, blends = (xh, xl), (ah, al), (bh, bl)

    def square(i, j):
        value = product(rows(xs, i), rows(xs, j), 1, 1)
        exact[part(i), part(j)] = value
        return value

    def blend(i, j):
        fourth = product(rows(squares, i), rows(squares, j), 1, 1)
        return COEFFS[1] * exact[part(i), part(j)] + COEFFS[2] * fourth

    for _ in range(NS_STEPS):
        symmetric(squares, square)
        symmetric(blends, blend)
        whole = (xh[...], xl[...])
        news = [COEFFS[0] * x[part(i), :] + product(rows(blends, i), whole) for i in range(2)]
        for i, new in enumerate(news):
            x[part(i), :] = new
            xh[part(i), :], xl[part(i), :] = halves(new)
    out[...] = x[...]


def orthogonal(place, chunks):
    size = chunks[0].shape[-1]
    return pl.pallas_call(
        orthogonal_kernel,
        out_shape=jax.ShapeDtypeStruct((size, size), F32),
        in_specs=[SMEM] + [VMEM] * RING,
        out_specs=VMEM,
        scratch_shapes=[pltpu.VMEM((size, size), F32)] * 2 + [pltpu.VMEM((size, size), BF16)] * 6,
        compiler_params=params(14),
        cost_estimate=pl.CostEstimate(
            flops=15 * 6 * size**3, bytes_accessed=8 * size * size, transcendentals=0
        ),
        name="orthogonal",
    )(place, *chunks)


def finish_kernel(picked, gate, gain, out):
    heads, _, size = picked.shape
    total = sum(jnp.sum(picked[h] * picked[h], axis=1, keepdims=True) for h in range(heads))
    scale = lax.rsqrt(total / (heads * size) + 1e-06)
    for h in range(heads):
        here = slice(h * size, (h + 1) * size)
        now = gate[:, here]
        out[:, here] = picked[h] * scale * gain[:, here] * (now * jax.nn.sigmoid(now))


def finish(picked, gate, gain):
    return pl.pallas_call(
        finish_kernel,
        out_shape=jax.ShapeDtypeStruct(gate.shape, F32),
        in_specs=[VMEM] * 3,
        out_specs=VMEM,
        compiler_params=params(10),
        cost_estimate=pl.CostEstimate(
            flops=8 * gate.size, bytes_accessed=12 * gate.size, transcendentals=gate.size
        ),
        name="finish",
    )(picked, gate, gain)


def apply_kernel(q_own, q_came, w1, w2, w3, result):
    queries = halves(jnp.concatenate([q_own[...], q_came[...]], axis=0))
    first = product(queries, halves(w1[...]))
    third = product(queries, halves(w3[...]))
    result[...] = product(halves(first * jax.nn.sigmoid(first) * third), halves(w2[...]))


def apply_fast(queries, weights):
    size = weights[0].shape[0]
    rows = 2 * queries[0].shape[0]
    return pl.pallas_call(
        apply_kernel,
        out_shape=jax.ShapeDtypeStruct((rows, size), F32),
        in_specs=[VMEM] * 5,
        out_specs=VMEM,
        compiler_params=params(16),
        cost_estimate=pl.CostEstimate(
            flops=18 * rows * size * size, bytes_accessed=16 * size * size, transcendentals=rows * size
        ),
        name="apply",
    )(*queries, *weights)


def plane_shift(value, dy, dz):
    pairs = [
        (y * RING + z, (y + dy) % RING * RING + (z + dz) % RING)
        for y in range(RING)
        for z in range(RING)
    ]
    return lax.ppermute(value, ("y", "z"), pairs)


def sum_to_diagonals(place, tops, lows):
    parts = [tops[0], lows[0]]
    for d in STEPS:
        parts += [plane_shift(tops[d], d, 0), plane_shift(lows[d], 0, d)]
    wanted = pick(place, parts)
    parts = list(wanted[:2])
    for d in STEPS:
        parts += [plane_shift(wanted[2 * d], 0, d), plane_shift(wanted[2 * d + 1], d, 0)]
    held = hold(parts)
    return [held] + [plane_shift(held, d, -d) for d in range(1, RING)]


def share(update):
    opposite = plane_shift(update, RING // 2, 0)
    return [update, plane_shift(update, 0, -1), opposite, plane_shift(update, 0, 1)]


def on_device(
    keys, values, queries, rates, w_first, w_second, w_third, step_size, owner_order, gate, gain
):
    size = w_first.shape[1]
    spans, rows = keys.shape[0], keys.shape[1]
    mine = lax.axis_index("xh")
    low_side = mine == 0
    heads = SIZES["xl"] * SIZES["core"]
    place = jnp.stack([lax.axis_index("y"), lax.axis_index("z")]).astype(jnp.int32)

    def sides(array):
        left, right = array[:, :size], array[:, size:]
        return jnp.where(low_side, left, right), jnp.where(low_side, right, left)

    kept, sent = sides(keys[0])
    sent, first_values = lax.optimization_barrier((sent, values[0]))
    now_keys = kept, shift(sent, "xh", 1)
    kept, sent = sides(first_values * rates[0][:, None])
    now_target = kept, shift(sent, "xh", 1)
    pieces = [queries[0]] + [
        piece for s in range(1, spans) for piece in (keys[s], values[s] * rates[s][:, None], queries[s])
    ]
    kept, sent = zip(*[sides(piece) for piece in pieces])
    order = owner_order[0]
    row = jnp.zeros((8, size), F32).at[0, : order.shape[0]].set(order.astype(F32))
    later, *first_came = lax.optimization_barrier(
        (jnp.concatenate(sent + (row,)), now_keys[1], now_target[1])
    )
    now_keys, now_target = (now_keys[0], first_came[0]), (now_target[0], first_came[1])
    came = shift(later, "xh", 1)
    other = came[rows * len(kept), : order.shape[0]].astype(jnp.int32)
    pairs = [(kept[n], came[rows * n : rows * (n + 1)]) for n in range(len(kept))]

    weights = [jnp.where(low_side, w[0], w[1]) for w in (w_first, w_second, w_third)]
    eta = jnp.where(low_side, step_size[:1], step_size[1:])
    outputs = []
    chunks = gradients(place, now_keys, now_target, weights)
    for span in range(spans):
        updates = share(orthogonal(place, sum_to_diagonals(place, *chunks)))
        now = pairs[3 * span]
        if span + 1 < spans:
            later = pairs[3 * span + 1], pairs[3 * span + 2]
            weights, *chunks = update_and_gradients(place, eta, *later, updates, weights)
            outputs.append(apply_fast(now, weights))
        else:
            outputs.append(update_and_apply(place, eta, now, updates, weights))
    results = jnp.concatenate(outputs, axis=0)

    def locate(tokens, block):
        return jnp.where(tokens < rows, tokens, tokens + rows) + block * rows

    here, there = locate(order, 0), locate(other, 1)
    low = jnp.where(low_side, here, there).reshape(heads, 1, -1)
    high = jnp.where(low_side, there, here).reshape(heads, 1, -1)
    index = jnp.concatenate([low, high], axis=1).reshape(-1)
    picked = jnp.take(results, index, axis=0)
    regrouped = lax.all_to_all(picked, ("xl", "core", "xh"), split_axis=0, concat_axis=0, tiled=True)
    return finish(regrouped.reshape(2 * heads, -1, size), gate[0], gain[None])[None]


def solution(mesh):
    split = Mesh(
        mesh.devices.reshape([count for _, count in SPLIT]), [name for name, _ in SPLIT]
    )
    in_specs = (
        P(None, CTX, HEAD),
        P(None, CTX, HEAD),
        P(None, CTX, HEAD),
        P(None, CTX),
        P(HEAD, None, None),
        P(HEAD, None, None),
        P(HEAD, None, None),
        P(HEAD),
        P(CTX, None),
        P(CTX, HEAD, None),
        P(),
    )
    out_specs = P(CTX, HEAD, None)
    return jax.shard_map(
        on_device, mesh=split, in_specs=in_specs, out_specs=out_specs, check_vma=False
    )
```
